32 devices in a mesh: row: 4 (over y, core), col: 8 (over z, x).
Axes of the slice: x: 2, y: 2, z: 4, core: 2. Of those that a mesh axis runs over, the one named last changes fastest.
Arguments:
- raster: bfloat16 [64, 128, 1024], P(None, 'row', 'col')
- conv_one: bfloat16 [64, 576], replicated, may hold values from -0.25 to 0.25
- bias_one: float32 [64], replicated, may hold values from -3 to 3
- conv_two: bfloat16 [64, 576], replicated, may hold values from -0.25 to 0.25
- bias_two: float32 [64], replicated, may hold values from -3 to 3
- pos_embed: bfloat16 [64, 4, 32], P(None, 'row', 'col'), may hold values from -6 to 6
- query_embed: bfloat16 [256, 256], replicated
- w_query: bfloat16 [256, 256], replicated, may hold values from -0.375 to 0.375
- w_key: bfloat16 [64, 256], replicated, may hold values from -0.75 to 0.75
- w_value: bfloat16 [64, 256], replicated, may hold values from -0.75 to 0.75
- w_out: bfloat16 [256, 256], replicated, may hold values from -0.375 to 0.375
- visible: int32 [2, 32], replicated, may hold values from 0 to 1, as said below
Outputs:
- map_queries: bfloat16 [256, 256], P(('row', 'col'))
The draws below stay inside these ranges and needn't reach their ends.
Inputs may be any that keep to these rules, and one draw needn't show every extreme that they name: `visible`: every query block sees at least one tile; each block sees a square of tiles around one tile and, independently, about one in eight of the other tiles.
All inputs are finite; a program needn't handle non-finite values.
Results may differ from the reference program's by a relative error of at most 0.035.
Values may be sent and summed in bfloat16 or wider, within the bound.
A program may use at most 128 MiB of HBM per device.

```python
import jax
import jax.numpy as jnp
from jax import lax

C = 64
E = 256
HEADS = 8
HEAD_DIM = 32
PATCH = 32
QBLOCK = 128
CELL_R = 32
CELL_C = 128
GRID_R = 128
GRID_C = 1024
PR = 4
PC = 32
QUERIES = 256
NQB = 2
TILES = 32
N_ROW = 4
N_COL = 8


def draw_raster(key, part):
    key_base = jax.random.fold_in(key, 11)
    key_gain = jax.random.fold_in(key, 12)
    key_shift = jax.random.fold_in(key, 13)
    blocks_r = GRID_R // 16
    blocks_c = GRID_C // 16
    gain = jnp.exp(jax.random.uniform(key_gain, (C, blocks_r, 1, blocks_c, 1), jnp.float32, -1.5, 1.5))
    shift = jnp.clip(0.7 * jax.random.normal(key_shift, (C, blocks_r, 1, blocks_c, 1), jnp.float32), -2.5, 2.5)
    base = jnp.clip(jax.random.normal(key_base, (C, blocks_r, 16, blocks_c, 16), jnp.float32), -6.0, 6.0)
    return (base * gain + shift).reshape(C, GRID_R, GRID_C).astype(jnp.bfloat16)


def draw_query_embed(key, part):
    key_base = jax.random.fold_in(key, 21)
    return (2.5 * jnp.clip(jax.random.normal(key_base, (QUERIES, E), jnp.float32), -6.0, 6.0)).astype(jnp.bfloat16)


def draw_visible(key, part):
    center_r = jax.random.randint(jax.random.fold_in(key, 31), (NQB, 1), 0, N_ROW)
    center_c = jax.random.randint(jax.random.fold_in(key, 32), (NQB, 1), 0, N_COL)
    radius = jax.random.randint(jax.random.fold_in(key, 33), (NQB, 1), 1, 4)
    extra = jax.random.randint(jax.random.fold_in(key, 34), (NQB, TILES), 0, 8) == 0
    tile_r = jnp.arange(TILES, dtype=jnp.int32)[None, :] // N_COL
    tile_c = jnp.arange(TILES, dtype=jnp.int32)[None, :] % N_COL
    reach = jnp.maximum(jnp.abs(tile_r - center_r), jnp.abs(tile_c - center_c))
    return ((reach <= radius) | extra).astype(jnp.int32)


def steps_of(own_key, dims, pieces, low, high):
    level, own = 1.0, jax.random.fold_in(own_key, 6)
    for position, shards_of in pieces:
        draws = jnp.exp(jax.random.uniform(jax.random.fold_in(own, position), (shards_of,), jnp.float32, low / len(pieces), high / len(pieces)))
        level = level * jnp.repeat(draws, dims[position] // shards_of).reshape([-1 if axis == position else 1 for axis in range(len(dims))])
    return level


def noise(key, dims, scale, bound, split=(), held_as=jnp.bfloat16):
    factor_of = steps_of(key, dims, split, -0.22, 0.18) if split else 1.0
    drawn = jax.random.normal(key, dims, jnp.float32) * scale * factor_of
    return jnp.minimum(jnp.maximum(drawn, -bound), bound).astype(held_as)


def setup_inputs(seed: int = 0) -> dict:
    seeds = jax.random.split(jax.random.key(seed), 13)
    return {
        "raster": draw_raster(jax.random.fold_in(seeds[12], 71), 0),
        "conv_one": noise(seeds[1], (C, 9 * C), (9 * C) ** -0.5, 0.25),
        "bias_one": noise(seeds[2], (C,), 0.5, 3.0, (), jnp.float32),
        "conv_two": noise(seeds[3], (C, 9 * C), (9 * C) ** -0.5, 0.25),
        "bias_two": noise(seeds[4], (C,), 0.5, 3.0, (), jnp.float32),
        "pos_embed": noise(seeds[5], (C, PR, PC), 1.0, 6.0, ((1, 4), (2, 8))),
        "query_embed": draw_query_embed(jax.random.fold_in(seeds[12], 71), 0),
        "w_query": noise(seeds[7], (E, E), E ** -0.5, 0.375),
        "w_key": noise(seeds[8], (C, E), C ** -0.5, 0.75),
        "w_value": noise(seeds[9], (C, E), C ** -0.5, 0.75),
        "w_out": noise(seeds[10], (E, E), E ** -0.5, 0.375),
        "visible": draw_visible(jax.random.fold_in(seeds[12], 71), 0),
    }


def conv_valid(padded, weight, bias):
    height = padded.shape[1] - 2
    width = padded.shape[2] - 2
    taps = [padded[:, dy:dy + height, dx:dx + width] for dy in range(3) for dx in range(3)]
    stacked = jnp.concatenate(taps, 0).astype(jnp.float32)
    out = jnp.einsum("ok,khw->ohw", weight.astype(jnp.float32), stacked) + bias[:, None, None]
    return jnp.maximum(out, 0.0)


def reference(raster, conv_one, bias_one, conv_two, bias_two, pos_embed, query_embed, w_query, w_key, w_value, w_out, visible):
    padded = jnp.pad(raster, ((0, 0), (2, 2), (2, 2)))

    def strip(index):
        start = (index * PATCH).astype(jnp.int32)
        piece = lax.dynamic_slice(padded, (jnp.int32(0), start, jnp.int32(0)), (C, PATCH + 4, GRID_C + 4))
        first = conv_valid(piece, conv_one, bias_one)
        rows_glob = start - 1 + jnp.arange(PATCH + 2, dtype=jnp.int32)
        cols_glob = jnp.arange(GRID_C + 2, dtype=jnp.int32) - 1
        inside = ((rows_glob >= 0) & (rows_glob < GRID_R))[:, None] & ((cols_glob >= 0) & (cols_glob < GRID_C))[None, :]
        first = jnp.where(inside[None], first, 0.0).astype(jnp.bfloat16)
        second = conv_valid(first, conv_two, bias_two)
        return second.reshape(C, PATCH, PC, PATCH).mean(axis=(1, 3))

    pooled = lax.map(strip, jnp.arange(PR, dtype=jnp.int32))
    pooled = jnp.transpose(pooled, (1, 0, 2))
    tokens = (pooled + pos_embed.astype(jnp.float32)).astype(jnp.bfloat16)
    flat = tokens.reshape(C, PR * PC).T
    keys = jnp.dot(flat, w_key, preferred_element_type=jnp.float32).astype(jnp.bfloat16)
    values = jnp.dot(flat, w_value, preferred_element_type=jnp.float32).astype(jnp.bfloat16)
    queries = jnp.dot(query_embed, w_query, preferred_element_type=jnp.float32).astype(jnp.bfloat16)
    patch_row = jnp.arange(PR * PC, dtype=jnp.int32) // PC
    patch_col = jnp.arange(PR * PC, dtype=jnp.int32) % PC
    tile_of = (patch_row // (CELL_R // PATCH)) * N_COL + patch_col // (CELL_C // PATCH)
    key_heads = keys.reshape(PR * PC, HEADS, HEAD_DIM).astype(jnp.float32)
    value_heads = values.reshape(PR * PC, HEADS, HEAD_DIM).astype(jnp.float32)
    scale = 1.0 / (HEAD_DIM ** 0.5)

    def block(index):
        query_rows = lax.dynamic_slice_in_dim(queries, (index * QBLOCK).astype(jnp.int32), QBLOCK, 0)
        query_heads = query_rows.reshape(QBLOCK, HEADS, HEAD_DIM).astype(jnp.float32)
        seen = visible[index][tile_of] > 0
        score = jnp.einsum("qhd,khd->hqk", query_heads, key_heads) * scale
        peak = jnp.max(jnp.where(seen[None, None, :], score, -1e30), axis=-1)
        weight = jnp.where(seen[None, None, :], jnp.exp(score - peak[..., None]), 0.0)
        total = jnp.sum(weight, axis=-1)
        mixed = jnp.einsum("hqk,khd->qhd", weight.astype(jnp.bfloat16).astype(jnp.float32), value_heads)
        attended = (mixed / total.T[:, :, None]).reshape(QBLOCK, E).astype(jnp.bfloat16)
        return jnp.dot(attended, w_out, preferred_element_type=jnp.float32).astype(jnp.bfloat16)

    result = lax.map(block, jnp.arange(NQB, dtype=jnp.int32))
    return result.reshape(QUERIES, E)
```

```python
import functools

import jax
import jax.numpy as jnp
from jax import lax
from jax.experimental import pallas as pl
from jax.experimental.pallas import tpu as pltpu
from jax.sharding import PartitionSpec as P

HEADS = 8
HEAD_DIM = 32
PATCH = 32
QBLOCK = 128
SLOT = 16
MESH = pl.DeviceIdType.MESH
F32 = jnp.float32
BF16 = jnp.bfloat16
SIDES = ((-1, -1), (-1, 1), (0, -1), (0, 1), (1, -1), (1, 1))


def iota(shape, dim):
    return lax.broadcasted_iota(jnp.int32, shape, dim)


def dot(a, b):
    return jnp.dot(a, b, preferred_element_type=F32)


def dot_nt(a, b):
    return lax.dot_general(a, b, (((1,), (1,)), ((), ())), preferred_element_type=F32)


def column(row_vec):
    n = row_vec.shape[1]
    spread = jnp.where(iota((n, n), 0) == iota((n, n), 1), row_vec, 0.0)
    return jnp.sum(spread, axis=1, keepdims=True)


def kernel(
    sizes,
    x_ref,
    conv_one_ref,
    bias_one_ref,
    conv_two_ref,
    bias_two_ref,
    pos_ref,
    embed_ref,
    w_query_ref,
    w_key_ref,
    w_value_ref,
    w_out_ref,
    visible_ref,
    out_ref,
    x3,
    f3,
    w2a,
    w2b,
    pack,
    rows_in,
    packs_in,
    token,
    gathered,
    row_send,
    row_recv,
    pack_send,
    pack_recv,
    tok_send,
    tok_recv,
):
    n_row, n_col, ch, rows, cols = sizes
    n = n_row * n_col
    r = lax.axis_index("row")
    c = lax.axis_index("col")
    me = r * n_col + c
    owned = out_ref.shape[0]
    e = out_ref.shape[1]

    def place(d):
        return (lax.div(d, n_col), lax.rem(d, n_col))

    barrier = pltpu.get_barrier_semaphore()

    def greet(k, carry):
        pl.semaphore_signal(
            barrier, inc=1, device_id=place(lax.rem(me + k, n)), device_id_type=MESH
        )
        return carry

    lax.fori_loop(1, n, greet, 0)

    lane = iota((ch, cols), 1)
    group = lax.rem(lane + 2, cols) // 4

    def pack_rows(i, acc):
        for j in range(4):
            h = i * 4 + j
            part = x_ref[pl.ds(pl.multiple_of(h * ch, ch), ch), :].astype(F32)
            acc = jnp.where(group == h, pltpu.roll(part, h * 4, 1), acc)
        return acc

    pack[...] = lax.fori_loop(0, rows // 4, pack_rows, jnp.zeros((ch, cols), F32)).astype(BF16)

    for conv_ref, w2 in ((conv_one_ref, w2a), (conv_two_ref, w2b)):
        w = conv_ref[...]
        pad = jnp.zeros((ch, 3 * ch), BF16)
        w2[0:ch, :] = jnp.concatenate([w, pad], axis=1)
        w2[ch : 2 * ch, :] = jnp.concatenate([pad, w], axis=1)

    pl.semaphore_wait(barrier, n - 1)

    def row_copy(up):
        return pltpu.make_async_remote_copy(
            src_ref=x_ref.at[pl.ds(0 if up else (rows - 2) * ch, 2 * ch)],
            dst_ref=rows_in.at[1 if up else 0],
            send_sem=row_send.at[0 if up else 1],
            recv_sem=row_recv.at[1 if up else 0],
            device_id=(r - 1 if up else r + 1, c),
            device_id_type=MESH,
        )

    def pack_copy(index):
        dr, dc = SIDES[index]
        there = SIDES.index((-dr, -dc))
        return pltpu.make_async_remote_copy(
            src_ref=pack,
            dst_ref=packs_in.at[there],
            send_sem=pack_send.at[index],
            recv_sem=pack_recv.at[there],
            device_id=(r + dr, c + dc),
            device_id_type=MESH,
        )

    def row_there(up):
        return r > 0 if up else r < n_row - 1

    def side_there(index):
        dr, dc = SIDES[index]
        ok = c > 0 if dc < 0 else c < n_col - 1
        if dr:
            ok = jnp.logical_and(ok, row_there(dr < 0))
        return ok

    for index in (2, 3, 0, 1, 4, 5):
        pl.when(side_there(index))(lambda index=index: pack_copy(index).start())
    for up in (True, False):
        pl.when(row_there(up))(lambda up=up: row_copy(up).start())

    pick = iota((owned, embed_ref.shape[0]), 1) == me * owned + iota((owned, embed_ref.shape[0]), 0)
    own = dot(pick.astype(F32).astype(BF16), embed_ref[...]).astype(BF16)
    query = dot(own, w_query_ref[...]).astype(BF16).astype(F32)
    tall = (HEADS * owned, e)
    own_head = iota(tall, 0) // owned == iota(tall, 1) // HEAD_DIM
    heads = jnp.where(own_head, jnp.concatenate([query] * HEADS, axis=0), 0.0).astype(BF16)
    wide = (visible_ref.shape[1], n * SLOT)
    local_count = pos_ref.shape[1]
    spread = jnp.logical_and(
        iota(wide, 1) // SLOT == iota(wide, 0), lax.rem(iota(wide, 1), SLOT) < local_count
    )
    blocks = visible_ref.shape
    mine = iota(blocks, 0) == me * owned // QBLOCK
    seen_row = jnp.sum(jnp.where(mine, visible_ref[...], 0).astype(F32), axis=0, keepdims=True)
    seen = dot(
        jnp.broadcast_to(seen_row, (8, blocks[1])).astype(BF16), spread.astype(F32).astype(BF16)
    )[0:1] > 0.5

    for index in range(6):

        @pl.when(side_there(index))
        def _(index=index):
            back = SIDES.index((-SIDES[index][0], -SIDES[index][1]))
            pack_copy(index).wait_send()
            pack_copy(back).wait_recv()

        @pl.when(jnp.logical_not(side_there(index)))
        def _(index=index):
            packs_in[index] = jnp.zeros((ch, cols), BF16)

    for up in (True, False):

        @pl.when(row_there(up))
        def _(up=up):
            row_copy(up).wait_send()
            row_copy(not up).wait_recv()

        @pl.when(jnp.logical_not(row_there(up)))
        def _(up=up):
            rows_in[0 if up else 1] = jnp.zeros((2 * ch, cols), BF16)

    from_right = lax.rem(lane, 4) < 2

    def rim(dr):
        left = packs_in[SIDES.index((dr, -1))].astype(F32)
        right = packs_in[SIDES.index((dr, 1))].astype(F32)
        return jnp.where(from_right, right, left)

    def fill(slot, center, rim_rolled):
        full = jnp.concatenate([center.astype(F32), rim_rolled], axis=1)
        base = pl.multiple_of(slot * (3 * ch), 3 * ch)
        x3[pl.ds(base, ch), :] = pltpu.roll(full, 1, 1).astype(BF16)
        x3[pl.ds(base + ch, ch), :] = full.astype(BF16)
        x3[pl.ds(base + 2 * ch, ch), :] = pltpu.roll(full, 2 * cols - 1, 1).astype(BF16)

    beside = rim(0)

    def fill_rows(i, carry):
        for j in range(4):
            h = i * 4 + j
            center = x_ref[pl.ds(pl.multiple_of(h * ch, ch), ch), :]
            fill(h + 2, center, pltpu.roll(beside, lax.rem(cols - 4 * h, cols), 1))
        return carry

    lax.fori_loop(0, rows // 4, fill_rows, 0)
    above, below = rim(-1), rim(1)
    for j in range(2):
        h = rows - 2 + j
        fill(j, rows_in[0, j * ch : (j + 1) * ch], pltpu.roll(above, (cols - 4 * h) % cols, 1))
        fill(rows + 2 + j, rows_in[1, j * ch : (j + 1) * ch], pltpu.roll(below, (cols - 4 * j) % cols, 1))

    bias_one = column(bias_one_ref[...])
    bias_two = column(bias_two_ref[...])
    bias_one = jnp.concatenate([bias_one, bias_one], axis=0)
    bias_two = jnp.concatenate([bias_two, bias_two], axis=0)
    lanes = iota((1, 2 * cols), 1)
    outside = jnp.logical_or(
        jnp.logical_and(lanes == 2 * cols - 1, c == 0),
        jnp.logical_and(lanes == cols, c == n_col - 1),
    )
    inside = jnp.logical_not(outside)
    half_row = iota((2 * ch, 1), 0) // ch
    lowest = jnp.where(r == 0, 0, -1)
    highest = jnp.where(r == n_row - 1, rows - 1, rows)
    half = rows // 2

    def first_pair(g, slot, side):
        base = pl.multiple_of(g * (6 * ch), 6 * ch)
        acc = dot(w2a[...], x3[pl.ds(base, 12 * ch), :])
        local = 2 * g - 1 + half_row
        keep = jnp.logical_and(jnp.logical_and(local >= lowest, local <= highest), inside)
        acc = jnp.where(keep, jnp.maximum(acc + bias_one, 0.0), 0.0)
        taps = (
            pltpu.roll(acc, 1, 1)[:, :cols].astype(BF16),
            acc[:, :cols].astype(BF16),
            pltpu.roll(acc, 2 * cols - 1, 1)[:, :cols].astype(BF16),
        )
        start = pl.multiple_of(slot * (6 * ch), 6 * ch)
        for o in range(2):
            for t in range(3):
                f3[pl.ds(start + (3 * o + t) * ch, ch), side * cols : (side + 1) * cols] = taps[t][
                    o * ch : (o + 1) * ch
                ]

    def first_step(i, carry):
        first_pair(i, i, 0)
        first_pair(i + half // 2, i, 1)
        return carry

    lax.fori_loop(0, half // 2 + 1, first_step, 0)

    def second_step(j, acc):
        base = pl.multiple_of(j * (6 * ch), 6 * ch)
        return acc + jnp.maximum(dot(w2b[...], f3[pl.ds(base, 12 * ch), :]) + bias_two, 0.0)

    total = lax.fori_loop(0, half // 2, second_step, jnp.zeros((2 * ch, 2 * cols), F32))
    total = total[:ch] + total[ch:]
    total = total[:, :cols] + total[:, cols:]
    high = total.astype(BF16)
    low = (total - high.astype(F32)).astype(BF16)
    pool = (iota((SLOT, cols), 1) // PATCH == iota((SLOT, cols), 0)).astype(F32).astype(BF16)
    pooled = (dot_nt(pool, high) + dot_nt(pool, low)) * (1.0 / (PATCH * PATCH))
    shift = (iota((SLOT, local_count), 1) == iota((SLOT, local_count), 0)).astype(F32).astype(BF16)
    tokens = pooled + dot_nt(shift, pos_ref[...])
    tokens = jnp.concatenate([tokens, jnp.zeros((SLOT, 128 - ch), F32)], axis=1).astype(BF16)
    token[...] = tokens
    gathered[pl.ds(pl.multiple_of(me * SLOT, SLOT), SLOT), :] = tokens

    def token_copy(k, sender):
        return pltpu.make_async_remote_copy(
            src_ref=token,
            dst_ref=gathered.at[pl.ds(pl.multiple_of(sender * SLOT, SLOT), SLOT)],
            send_sem=tok_send.at[k],
            recv_sem=tok_recv.at[sender],
            device_id=place(lax.rem(me + k, n)),
            device_id_type=MESH,
        )

    def push(k, carry):
        token_copy(k, me).start()
        return carry

    def take(k, carry):
        token_copy(k, me).wait_send()
        token_copy(k, lax.rem(me + n - k, n)).wait_recv()
        return carry

    lax.fori_loop(1, n, push, 0)
    lax.fori_loop(1, n, take, 0)

    every = gathered[...][:, :ch]
    keys = dot(every, w_key_ref[...]).astype(BF16)
    values = dot(every, w_value_ref[...]).astype(BF16)
    score = dot_nt(heads, keys) * (1.0 / HEAD_DIM**0.5)
    peak = jnp.max(jnp.where(seen, score, -1e30), axis=1, keepdims=True)
    weight = jnp.where(seen, jnp.exp(score - peak), 0.0)
    norm = jnp.sum(weight, axis=1, keepdims=True)
    mixed = dot(weight.astype(BF16), values) / norm
    mixed = jnp.where(own_head, mixed, 0.0)
    attended = mixed[0:owned]
    for h in range(1, HEADS):
        attended = attended + mixed[h * owned : (h + 1) * owned]
    out_ref[...] = dot(attended.astype(BF16), w_out_ref[...]).astype(BF16)


def on_device(
    raster,
    conv_one,
    bias_one,
    conv_two,
    bias_two,
    pos_embed,
    query_embed,
    w_query,
    w_key,
    w_value,
    w_out,
    visible,
):
    ch, rows, cols = raster.shape
    n_row, n_col = lax.axis_size("row"), lax.axis_size("col")
    n = n_row * n_col
    owned = query_embed.shape[0] // n
    e = query_embed.shape[1]
    flat = raster.transpose(1, 0, 2).reshape(rows * ch, cols)
    vmem = pl.BlockSpec(memory_space=pltpu.VMEM)
    dma = pltpu.SemaphoreType.DMA
    return pl.pallas_call(
        functools.partial(kernel, (n_row, n_col, ch, rows, cols)),
        out_shape=jax.ShapeDtypeStruct((owned, e), BF16),
        in_specs=[vmem] * 12,
        out_specs=vmem,
        scratch_shapes=[
            pltpu.VMEM(((rows + 4) * 3 * ch, 2 * cols), BF16),
            pltpu.VMEM(((rows // 2 + 2) * 3 * ch, 2 * cols), BF16),
            pltpu.VMEM((2 * ch, 12 * ch), BF16),
            pltpu.VMEM((2 * ch, 12 * ch), BF16),
            pltpu.VMEM((ch, cols), BF16),
            pltpu.VMEM((2, 2 * ch, cols), BF16),
            pltpu.VMEM((6, ch, cols), BF16),
            pltpu.VMEM((SLOT, 128), BF16),
            pltpu.VMEM((n * SLOT, 128), BF16),
            dma((2,)),
            dma((2,)),
            dma((6,)),
            dma((6,)),
            dma((n,)),
            dma((n,)),
        ],
        compiler_params=pltpu.CompilerParams(
            collective_id=0, has_side_effects=True, vmem_limit_bytes=40 * 1024 * 1024
        ),
        cost_estimate=pl.CostEstimate(flops=1_000_000_000, bytes_accessed=2_000_000, transcendentals=0),
    )(
        flat,
        conv_one,
        bias_one.reshape(1, ch),
        conv_two,
        bias_two.reshape(1, ch),
        pos_embed.reshape(ch, -1),
        query_embed,
        w_query,
        w_key,
        w_value,
        w_out,
        visible,
    )


def solution(mesh):
    tile = P(None, "row", "col")
    in_specs = (tile, P(), P(), P(), P(), tile, P(), P(), P(), P(), P(), P())
    return jax.shard_map(
        on_device,
        mesh=mesh,
        in_specs=in_specs,
        out_specs=P(("row", "col"), None),
        check_vma=False,
    )
```

```python
import functools

import jax
import jax.numpy as jnp
from jax import lax
from jax.experimental import pallas as pl
from jax.experimental.pallas import tpu as pltpu
from jax.sharding import PartitionSpec as P

HEADS = 8
HEAD_DIM = 32
PATCH = 32
QBLOCK = 128
SLOT = 16
MESH = pl.DeviceIdType.MESH
F32 = jnp.float32
BF16 = jnp.bfloat16
SIDES = ((0, -1), (0, 1), (-1, 0), (1, 0), (-1, -1), (-1, 1), (1, -1), (1, 1))


def iota(shape, dim):
    return lax.broadcasted_iota(jnp.int32, shape, dim)


def dot(a, b):
    return jnp.dot(a, b, preferred_element_type=F32)


def dot_nt(a, b):
    return lax.dot_general(a, b, (((1,), (1,)), ((), ())), preferred_element_type=F32)


def column(row_vec):
    n = row_vec.shape[1]
    spread = jnp.where(iota((n, n), 0) == iota((n, n), 1), row_vec, 0.0)
    return jnp.sum(spread, axis=1, keepdims=True)


def kernel(sizes, *refs):
    n_row, n_col, ch, rows, cols = sizes
    operands, out_ref, local = refs[:12], refs[12], refs[13:25]
    (xt, x3, f3, w2a, w2b, pack, rows_in, packs_in, token, gathered) = refs[25:35]
    (load_sem, row_send, row_recv, pack_send, pack_recv, tok_send, tok_recv) = refs[35:]
    (
        raster_ref,
        conv_one_ref,
        bias_one_ref,
        conv_two_ref,
        bias_two_ref,
        pos_ref,
        embed_ref,
        w_query_ref,
        w_key_ref,
        w_value_ref,
        w_out_ref,
        visible_ref,
    ) = local
    n = n_row * n_col
    r = lax.axis_index("row")
    c = lax.axis_index("col")
    me = r * n_col + c
    owned = out_ref.shape[0]
    e = out_ref.shape[1]
    half = rows // 2

    loads = [
        pltpu.make_async_copy(operands[i], local[i], load_sem.at[i]) for i in range(len(operands))
    ]
    loads[0].start()

    def away(i, j):
        rr, cc = r + i, c + j
        return (jnp.where(rr >= n_row, rr - n_row, rr), jnp.where(cc >= n_col, cc - n_col, cc))

    def others(body):
        for i in range(n_row):
            lax.fori_loop(0 if i else 1, n_col, lambda j, carry, i=i: body(i, j, carry), 0)

    barrier = pltpu.get_barrier_semaphore()

    def greet(i, j, carry):
        pl.semaphore_signal(barrier, inc=1, device_id=away(i, j), device_id_type=MESH)
        return carry

    others(greet)
    for copy in loads[1:]:
        copy.start()

    loads[0].wait()

    def turn(i, carry):
        start = pl.multiple_of(i * 16, 16)
        part = raster_ref[pl.ds(start, 16)].astype(F32)
        part = jnp.transpose(part, (1, 0, 2)).astype(BF16)
        xt[:, pl.ds(start, 16), :] = part
        return carry

    lax.fori_loop(0, ch // 16, turn, 0)

    lane = iota((ch, cols), 1)
    group = lax.rem(lane + 2, cols) // 4

    def pack_rows(i, acc):
        for j in range(4):
            h = i * 4 + j
            acc = jnp.where(group == h, pltpu.roll(xt[h].astype(F32), h * 4, 1), acc)
        return acc

    packed = lax.fori_loop(0, rows // 4, pack_rows, jnp.zeros((ch, cols), F32))
    pack[...] = packed.astype(BF16)

    pl.semaphore_wait(barrier, n - 1)

    def row_copy(up):
        return pltpu.make_async_remote_copy(
            src_ref=xt.at[pl.ds(0 if up else rows - 2, 2)],
            dst_ref=rows_in.at[1 if up else 0],
            send_sem=row_send.at[0 if up else 1],
            recv_sem=row_recv.at[1 if up else 0],
            device_id=(r - 1 if up else r + 1, c),
            device_id_type=MESH,
        )

    def pack_copy(index):
        dr, dc = SIDES[index]
        there = SIDES.index((-dr, -dc))
        return pltpu.make_async_remote_copy(
            src_ref=pack,
            dst_ref=packs_in.at[there],
            send_sem=pack_send.at[index],
            recv_sem=pack_recv.at[there],
            device_id=(r + dr, c + dc),
            device_id_type=MESH,
        )

    def row_there(up):
        return r > 0 if up else r < n_row - 1

    def side_there(index):
        dr, dc = SIDES[index]
        ok = None
        if dr:
            ok = row_there(dr < 0)
        if dc:
            beside = c > 0 if dc < 0 else c < n_col - 1
            ok = beside if ok is None else jnp.logical_and(ok, beside)
        return ok

    for up in (True, False):
        pl.when(row_there(up))(lambda up=up: row_copy(up).start())
    for index in range(8):
        pl.when(side_there(index))(lambda index=index: pack_copy(index).start())

    for copy in loads[1:]:
        copy.wait()

    for conv_ref, w2 in ((conv_one_ref, w2a), (conv_two_ref, w2b)):
        w = conv_ref[...]
        pad = jnp.zeros((ch, 3 * ch), BF16)
        w2[0:ch, :] = jnp.concatenate([w, pad], axis=1)
        w2[ch : 2 * ch, :] = jnp.concatenate([pad, w], axis=1)

    pick = iota((owned, embed_ref.shape[0]), 1) == me * owned + iota((owned, embed_ref.shape[0]), 0)
    own = dot(pick.astype(F32).astype(BF16), embed_ref[...]).astype(BF16)
    query = dot(own, w_query_ref[...]).astype(BF16).astype(F32)
    tall = (HEADS * owned, e)
    own_head = iota(tall, 0) // owned == iota(tall, 1) // HEAD_DIM
    heads = jnp.where(own_head, jnp.concatenate([query] * HEADS, axis=0), 0.0).astype(BF16)
    wide = (visible_ref.shape[1], n * SLOT)
    local_count = pos_ref.shape[0]
    spread = jnp.logical_and(
        iota(wide, 1) // SLOT == iota(wide, 0), lax.rem(iota(wide, 1), SLOT) < local_count
    )
    blocks = visible_ref.shape
    mine = iota(blocks, 0) == me * owned // QBLOCK
    seen_row = jnp.sum(jnp.where(mine, visible_ref[...], 0).astype(F32), axis=0, keepdims=True)
    seen = dot(
        jnp.broadcast_to(seen_row, (8, blocks[1])).astype(BF16), spread.astype(F32).astype(BF16)
    )[0:1] > 0.5

    bias_one = column(bias_one_ref[...])
    bias_two = column(bias_two_ref[...])
    bias_pair = jnp.concatenate([bias_one, bias_one], axis=0)
    bias_two = jnp.concatenate([bias_two, bias_two], axis=0)

    for up in (True, False):

        @pl.when(row_there(up))
        def _(up=up):
            row_copy(up).wait_send()
            row_copy(not up).wait_recv()

        @pl.when(jnp.logical_not(row_there(up)))
        def _(up=up):
            rows_in[0 if up else 1] = jnp.zeros((2, ch, cols), BF16)

    for index in range(8):

        @pl.when(side_there(index))
        def _(index=index):
            back = SIDES.index((-SIDES[index][0], -SIDES[index][1]))
            pack_copy(index).wait_send()
            pack_copy(back).wait_recv()

        @pl.when(jnp.logical_not(side_there(index)))
        def _(index=index):
            packs_in[index] = jnp.zeros((ch, cols), BF16)

    at_left = lax.rem(lane, 4) == 0

    def turned(x, shift):
        return pltpu.roll(x, shift % cols, 1)

    def rim(dr):
        left = packs_in[SIDES.index((dr, -1))].astype(F32)
        right = packs_in[SIDES.index((dr, 1))].astype(F32)
        mid = packs_in[SIDES.index((dr, 0))].astype(F32) if dr else packed
        return (
            jnp.where(at_left, turned(left, 2), mid),
            jnp.where(at_left, turned(left, 1), turned(right, -1)),
            jnp.where(at_left, mid, turned(right, -2)),
        )

    above, beside, below = rim(-1), rim(0), rim(1)

    def fill(slot, side, center, edge):
        left = jnp.where(lane == 0, edge, pltpu.roll(center, 1, 1))
        right = jnp.where(lane == cols - 1, edge, pltpu.roll(center, cols - 1, 1))
        base = slot * (3 * ch)
        if not isinstance(slot, int):
            base = pl.multiple_of(base, 3 * ch)
        where = slice(side * cols, (side + 1) * cols)
        for t, part in enumerate((left, center, right)):
            x3[pl.ds(base + t * ch, ch), where] = part.astype(BF16)

    def fill_rows(i, carry):
        for j in range(2):
            for side in range(2):
                s = i * 2 + j
                h = s + side * (half - 2)
                fill(s + 2 - 2 * side, side, xt[h].astype(F32), pltpu.roll(beside[1], lax.rem(cols - 4 * h + cols, cols), 1))
        return carry

    lax.fori_loop(0, half // 2 + 1, fill_rows, 0)
    for j in range(2):
        fill(j, 0, rows_in[0, j].astype(F32), turned(above[1], -4 * (rows - 2 + j)))
        fill(half + 2 + j, 1, rows_in[1, j].astype(F32), turned(below[1], -4 * j))

    row_of = lax.rem(lane + 1, cols) // 4
    first_row, last_row = row_of == 0, row_of == rows - 1
    main, extra = [], []
    for t in range(3):
        up_above, up_own = turned(above[t], 4), turned(beside[t], 4)
        main.append(jnp.where(first_row, up_above, up_own))
        extra.append(jnp.where(last_row, up_above, up_own))
    for t in range(3):
        main.append(beside[t])
        extra.append(jnp.where(last_row, above[t], below[t]))
    for t in range(3):
        down_below, down_own = turned(below[t], -4), turned(beside[t], -4)
        main.append(jnp.where(last_row, down_below, down_own))
        extra.append(jnp.where(last_row, down_own, down_below))
    taps = jnp.concatenate(
        [jnp.concatenate(main, axis=0).astype(BF16), jnp.concatenate(extra, axis=0).astype(BF16)], axis=1
    )
    edge = jnp.maximum(dot(conv_one_ref[...], taps) + bias_one, 0.0)
    outside = jnp.logical_or(
        jnp.logical_and(at_left, c == 0), jnp.logical_and(jnp.logical_not(at_left), c == n_col - 1)
    )
    off_grid = jnp.logical_or(
        jnp.logical_and(last_row, r == 0), jnp.logical_and(jnp.logical_not(last_row), r == n_row - 1)
    )
    edge_main = jnp.where(outside, 0.0, edge[:, :cols])
    edge_extra = jnp.where(jnp.logical_or(outside, off_grid), 0.0, edge[:, cols:])

    def put(pair, side, acc, edges):
        for o in range(2):
            part = acc[o * ch : (o + 1) * ch, side * cols : (side + 1) * cols]
            left = jnp.where(lane == 0, edges[o], pltpu.roll(part, 1, 1))
            right = jnp.where(lane == cols - 1, edges[o], pltpu.roll(part, cols - 1, 1))
            base = pair * (6 * ch)
            if not isinstance(pair, int):
                base = pl.multiple_of(base, 6 * ch)
            for t, piece in enumerate((left, part, right)):
                f3[pl.ds(base + (3 * o + t) * ch, ch), side * cols : (side + 1) * cols] = piece.astype(
                    BF16
                )

    def first_pair(i):
        base = i * (6 * ch)
        if not isinstance(i, int):
            base = pl.multiple_of(base, 6 * ch)
        return jnp.maximum(dot(w2a[...], x3[pl.ds(base, 12 * ch), :]) + bias_pair, 0.0)

    def edge_of(h):
        return pltpu.roll(edge_main, lax.rem(2 * cols - 4 * h, cols), 1)

    top = jnp.logical_and(iota((2 * ch, 2 * cols), 0) < ch, iota((2 * ch, 2 * cols), 1) < cols)
    acc = jnp.where(jnp.logical_and(top, r == 0), 0.0, first_pair(0))
    put(0, 0, acc, (turned(edge_extra, -4 * (rows - 1)), turned(edge_main, 0)))
    put(0, 1, acc, (turned(edge_main, -4 * (half - 1)), turned(edge_main, -4 * half)))

    def first_step(i, carry):
        acc = first_pair(i)
        for side in range(2):
            h = 2 * i - 1 + side * half
            put(i, side, acc, (edge_of(h), edge_of(h + 1)))
        return carry

    lax.fori_loop(1, half // 2, first_step, 0)
    bottom = jnp.logical_and(iota((2 * ch, 2 * cols), 0) >= ch, iota((2 * ch, 2 * cols), 1) >= cols)
    acc = jnp.where(jnp.logical_and(bottom, r == n_row - 1), 0.0, first_pair(half // 2))
    put(half // 2, 0, acc, (turned(edge_main, -4 * (half - 1)), turned(edge_main, -4 * half)))
    put(half // 2, 1, acc, (turned(edge_main, -4 * (rows - 1)), turned(edge_extra, 0)))

    def second_step(j, acc):
        base = pl.multiple_of(j * (6 * ch), 6 * ch)
        return acc + jnp.maximum(dot(w2b[...], f3[pl.ds(base, 12 * ch), :]) + bias_two, 0.0)

    total = lax.fori_loop(0, half // 2, second_step, jnp.zeros((2 * ch, 2 * cols), F32))
    total = total[:ch] + total[ch:]
    total = total[:, :cols] + total[:, cols:]
    high = total.astype(BF16)
    low = (total - high.astype(F32)).astype(BF16)
    pool = (iota((SLOT, cols), 1) // PATCH == iota((SLOT, cols), 0)).astype(F32).astype(BF16)
    pooled = (dot_nt(pool, high) + dot_nt(pool, low)) * (1.0 / (PATCH * PATCH))
    shift = jnp.concatenate(
        [pos_ref[...].astype(F32), jnp.zeros((SLOT - local_count, ch), F32)], axis=0
    )
    tokens = jnp.concatenate([pooled + shift, jnp.zeros((SLOT, 128 - ch), F32)], axis=1).astype(BF16)
    token[...] = tokens
    gathered[pl.ds(pl.multiple_of(me * SLOT, SLOT), SLOT), :] = tokens

    def token_copy(i, j, sender):
        return pltpu.make_async_remote_copy(
            src_ref=token,
            dst_ref=gathered.at[pl.ds(pl.multiple_of(sender * SLOT, SLOT), SLOT)],
            send_sem=tok_send.at[i * n_col + j],
            recv_sem=tok_recv.at[sender],
            device_id=away(i, j),
            device_id_type=MESH,
        )

    def push(i, j, carry):
        token_copy(i, j, me).start()
        return carry

    def take(i, j, carry):
        token_copy(i, j, me).wait_send()
        rr, cc = away(i, j)
        token_copy(i, j, rr * n_col + cc).wait_recv()
        return carry

    others(push)
    others(take)

    every = gathered[...][:, :ch]
    keys = dot(every, w_key_ref[...]).astype(BF16)
    values = dot(every, w_value_ref[...]).astype(BF16)
    score = dot_nt(heads, keys) * (1.0 / HEAD_DIM**0.5)
    peak = jnp.max(jnp.where(seen, score, -1e30), axis=1, keepdims=True)
    weight = jnp.where(seen, jnp.exp(score - peak), 0.0)
    norm = jnp.sum(weight, axis=1, keepdims=True)
    mixed = dot(weight.astype(BF16), values) / norm
    mixed = jnp.where(own_head, mixed, 0.0)
    attended = mixed[0:owned]
    for h in range(1, HEADS):
        attended = attended + mixed[h * owned : (h + 1) * owned]
    out_ref[...] = dot(attended.astype(BF16), w_out_ref[...]).astype(BF16)


def on_device(
    raster,
    conv_one,
    bias_one,
    conv_two,
    bias_two,
    pos_embed,
    query_embed,
    w_query,
    w_key,
    w_value,
    w_out,
    visible,
):
    ch, rows, cols = raster.shape
    n_row, n_col = lax.axis_size("row"), lax.axis_size("col")
    n = n_row * n_col
    owned = query_embed.shape[0] // n
    e = query_embed.shape[1]
    dma = pltpu.SemaphoreType.DMA
    operands = (
        raster,
        conv_one,
        bias_one.reshape(1, ch),
        conv_two,
        bias_two.reshape(1, ch),
        pos_embed.transpose(1, 2, 0).reshape(-1, ch),
        query_embed,
        w_query,
        w_key,
        w_value,
        w_out,
        visible,
    )
    wide = 3 * ch, 2 * cols
    return pl.pallas_call(
        functools.partial(kernel, (n_row, n_col, ch, rows, cols)),
        out_shape=jax.ShapeDtypeStruct((owned, e), BF16),
        in_specs=[pl.BlockSpec(memory_space=pl.ANY)] * len(operands),
        out_specs=pl.BlockSpec(memory_space=pltpu.VMEM),
        scratch_shapes=[pltpu.VMEM(x.shape, x.dtype) for x in operands]
        + [
            pltpu.VMEM((rows, ch, cols), BF16),
            pltpu.VMEM(((rows // 2 + 4) * wide[0], wide[1]), BF16),
            pltpu.VMEM(((rows // 2 + 2) * wide[0], wide[1]), BF16),
            pltpu.VMEM((2 * ch, 12 * ch), BF16),
            pltpu.VMEM((2 * ch, 12 * ch), BF16),
            pltpu.VMEM((ch, cols), BF16),
            pltpu.VMEM((2, 2, ch, cols), BF16),
            pltpu.VMEM((8, ch, cols), BF16),
            pltpu.VMEM((SLOT, 128), BF16),
            pltpu.VMEM((n * SLOT, 128), BF16),
            dma((len(operands),)),
            dma((2,)),
            dma((2,)),
            dma((8,)),
            dma((8,)),
            dma((n,)),
            dma((n,)),
        ],
        compiler_params=pltpu.CompilerParams(
            collective_id=0, has_side_effects=True, vmem_limit_bytes=62 * 1024 * 1024
        ),
        cost_estimate=pl.CostEstimate(flops=1_000_000_000, bytes_accessed=2_000_000, transcendentals=0),
    )(*operands)


def solution(mesh):
    tile = P(None, "row", "col")
    in_specs = (tile, P(), P(), P(), P(), tile, P(), P(), P(), P(), P(), P())
    return jax.shard_map(
        on_device,
        mesh=mesh,
        in_specs=in_specs,
        out_specs=P(("row", "col"), None),
        check_vma=False,
    )
```

```python
import functools

import jax
import jax.numpy as jnp
from jax import lax
from jax.experimental import pallas as pl
from jax.experimental.pallas import tpu as pltpu
from jax.sharding import PartitionSpec as P

HEADS = 8
HEAD_DIM = 32
PATCH = 32
QBLOCK = 128
SLOT = 16
MESH = pl.DeviceIdType.MESH
F32 = jnp.float32
BF16 = jnp.bfloat16
SIDES = ((0, -1), (0, 1), (-1, 0), (1, 0), (-1, -1), (-1, 1), (1, -1), (1, 1))


def iota(shape, dim):
    return lax.broadcasted_iota(jnp.int32, shape, dim)


def dot(a, b):
    return jnp.dot(a, b, preferred_element_type=F32)


def dot_nt(a, b):
    return lax.dot_general(a, b, (((1,), (1,)), ((), ())), preferred_element_type=F32)


def column(row_vec):
    n = row_vec.shape[1]
    spread = jnp.where(iota((n, n), 0) == iota((n, n), 1), row_vec, 0.0)
    return jnp.sum(spread, axis=1, keepdims=True)


def kernel(sizes, *refs):
    n_row, n_col, ch, rows, cols = sizes
    operands, out_ref, local = refs[:12], refs[12], refs[13:25]
    (xt, x3, raw, f3, w2a, w2b, pack, rows_in, packs_in, token, gathered) = refs[25:36]
    (load_sem, row_send, row_recv, pack_send, pack_recv, tok_send, tok_recv) = refs[36:]
    (
        raster_ref,
        conv_one_ref,
        bias_one_ref,
        conv_two_ref,
        bias_two_ref,
        pos_ref,
        embed_ref,
        w_query_ref,
        w_key_ref,
        w_value_ref,
        w_out_ref,
        visible_ref,
    ) = local
    n = n_row * n_col
    r = lax.axis_index("row")
    c = lax.axis_index("col")
    me = r * n_col + c
    owned = out_ref.shape[0]
    e = out_ref.shape[1]
    half = rows // 2

    chunk = ch // 4
    raster_loads = [
        pltpu.make_async_copy(
            operands[0].at[pl.ds(i * chunk, chunk)], raster_ref.at[pl.ds(i * chunk, chunk)], load_sem.at[i]
        )
        for i in range(4)
    ]
    loads = [
        pltpu.make_async_copy(operands[i], local[i], load_sem.at[i + 3]) for i in range(1, len(operands))
    ]
    for copy in raster_loads:
        copy.start()

    def away(i, j):
        rr, cc = r + i, c + j
        return (jnp.where(rr >= n_row, rr - n_row, rr), jnp.where(cc >= n_col, cc - n_col, cc))

    def others(body):
        for i in range(n_row):
            lax.fori_loop(0 if i else 1, n_col, lambda j, carry, i=i: body(i, j, carry), 0)

    barrier = pltpu.get_barrier_semaphore()

    def greet(i, j, carry):
        pl.semaphore_signal(barrier, inc=1, device_id=away(i, j), device_id_type=MESH)
        return carry

    others(greet)
    for copy in loads:
        copy.start()

    for i, copy in enumerate(raster_loads):
        copy.wait()
        part = raster_ref[i * chunk : (i + 1) * chunk].astype(F32)
        xt[:, i * chunk : (i + 1) * chunk, :] = jnp.transpose(part, (1, 0, 2)).astype(BF16)

    lane = iota((ch, cols), 1)
    group = lax.rem(lane + 2, cols) // 4

    def pack_rows(i, acc):
        for j in range(4):
            h = i * 4 + j
            acc = jnp.where(group == h, pltpu.roll(xt[h].astype(F32), h * 4, 1), acc)
        return acc

    packed = lax.fori_loop(0, rows // 4, pack_rows, jnp.zeros((ch, cols), F32))
    pack[...] = packed.astype(BF16)

    pl.semaphore_wait(barrier, n - 1)

    def row_copy(up):
        return pltpu.make_async_remote_copy(
            src_ref=xt.at[pl.ds(0 if up else rows - 2, 2)],
            dst_ref=rows_in.at[1 if up else 0],
            send_sem=row_send.at[0 if up else 1],
            recv_sem=row_recv.at[1 if up else 0],
            device_id=(r - 1 if up else r + 1, c),
            device_id_type=MESH,
        )

    def pack_copy(index):
        dr, dc = SIDES[index]
        there = SIDES.index((-dr, -dc))
        return pltpu.make_async_remote_copy(
            src_ref=pack,
            dst_ref=packs_in.at[there],
            send_sem=pack_send.at[index],
            recv_sem=pack_recv.at[there],
            device_id=(r + dr, c + dc),
            device_id_type=MESH,
        )

    def row_there(up):
        return r > 0 if up else r < n_row - 1

    def side_there(index):
        dr, dc = SIDES[index]
        ok = None
        if dr:
            ok = row_there(dr < 0)
        if dc:
            beside = c > 0 if dc < 0 else c < n_col - 1
            ok = beside if ok is None else jnp.logical_and(ok, beside)
        return ok

    for up in (True, False):
        pl.when(row_there(up))(lambda up=up: row_copy(up).start())
    for index in range(8):
        pl.when(side_there(index))(lambda index=index: pack_copy(index).start())

    for copy in loads:
        copy.wait()

    for conv_ref, w2 in ((conv_one_ref, w2a), (conv_two_ref, w2b)):
        w = conv_ref[...]
        pad = jnp.zeros((ch, 3 * ch), BF16)
        w2[0:ch, :] = jnp.concatenate([w, pad], axis=1)
        w2[ch : 2 * ch, :] = jnp.concatenate([pad, w], axis=1)

    def fill(slot, side, center):
        left = jnp.where(lane == 0, 0.0, pltpu.roll(center, 1, 1))
        right = jnp.where(lane == cols - 1, 0.0, pltpu.roll(center, cols - 1, 1))
        base = slot * (3 * ch)
        if not isinstance(slot, int):
            base = pl.multiple_of(base, 3 * ch)
        where = slice(side * cols, (side + 1) * cols)
        for t, part in enumerate((left, center, right)):
            x3[pl.ds(base + t * ch, ch), where] = part.astype(BF16)

    def fill_rows(i, carry):
        for j in range(2):
            for side in range(2):
                s = i * 2 + j
                fill(s + 2 - 2 * side, side, xt[s + side * (half - 2)].astype(F32))
        return carry

    lax.fori_loop(0, half // 2 + 1, fill_rows, 0)

    def first_sums(i, carry):
        base = i * (6 * ch)
        out = i * (2 * ch)
        if not isinstance(i, int):
            base, out = pl.multiple_of(base, 6 * ch), pl.multiple_of(out, 2 * ch)
        raw[pl.ds(out, 2 * ch), :] = dot(w2a[...], x3[pl.ds(base, 12 * ch), :])
        return carry

    lax.fori_loop(1, half // 2, first_sums, 0)

    pick = iota((owned, embed_ref.shape[0]), 1) == me * owned + iota((owned, embed_ref.shape[0]), 0)
    own = dot(pick.astype(F32).astype(BF16), embed_ref[...]).astype(BF16)
    query = dot(own, w_query_ref[...]).astype(BF16).astype(F32)
    tall = (HEADS * owned, e)
    own_head = iota(tall, 0) // owned == iota(tall, 1) // HEAD_DIM
    heads = jnp.where(own_head, jnp.concatenate([query] * HEADS, axis=0), 0.0).astype(BF16)
    local_count = pos_ref.shape[0]
    wide = (visible_ref.shape[1], n * local_count)
    spread = iota(wide, 1) // local_count == iota(wide, 0)
    blocks = visible_ref.shape
    mine = iota(blocks, 0) == me * owned // QBLOCK
    seen_row = jnp.sum(jnp.where(mine, visible_ref[...], 0).astype(F32), axis=0, keepdims=True)
    seen = dot(
        jnp.broadcast_to(seen_row, (8, blocks[1])).astype(BF16), spread.astype(F32).astype(BF16)
    )[0:1] > 0.5

    bias_one = column(bias_one_ref[...])
    bias_two = column(bias_two_ref[...])
    bias_two = jnp.concatenate([bias_two, bias_two], axis=0)

    for up in (True, False):

        @pl.when(row_there(up))
        def _(up=up):
            row_copy(up).wait_send()
            row_copy(not up).wait_recv()

        @pl.when(jnp.logical_not(row_there(up)))
        def _(up=up):
            rows_in[0 if up else 1] = jnp.zeros((2, ch, cols), BF16)

    for index in range(8):

        @pl.when(side_there(index))
        def _(index=index):
            back = SIDES.index((-SIDES[index][0], -SIDES[index][1]))
            pack_copy(index).wait_send()
            pack_copy(back).wait_recv()

        @pl.when(jnp.logical_not(side_there(index)))
        def _(index=index):
            packs_in[index] = jnp.zeros((ch, cols), BF16)

    at_left = lax.rem(lane, 4) == 0

    def turned(x, shift):
        return pltpu.roll(x, shift % cols, 1)

    def rim(dr):
        left = packs_in[SIDES.index((dr, -1))].astype(F32)
        right = packs_in[SIDES.index((dr, 1))].astype(F32)
        mid = packs_in[SIDES.index((dr, 0))].astype(F32) if dr else packed
        return (
            jnp.where(at_left, turned(left, 2), mid),
            jnp.where(at_left, turned(left, 1), turned(right, -1)),
            jnp.where(at_left, mid, turned(right, -2)),
        )

    above, beside, below = rim(-1), rim(0), rim(1)

    for j in range(2):
        fill(j, 0, rows_in[0, j].astype(F32))
        fill(half + 2 + j, 1, rows_in[1, j].astype(F32))
    first_sums(0, 0)
    first_sums(half // 2, 0)

    row_of = lax.rem(lane + 1, cols) // 4
    first_row, last_row = row_of == 0, row_of == rows - 1
    main, extra = [], []
    for t in range(3):
        up_above, up_own = turned(above[t], 4), turned(beside[t], 4)
        main.append(jnp.where(first_row, up_above, up_own))
        extra.append(jnp.where(last_row, up_above, up_own))
    for t in range(3):
        main.append(beside[t])
        extra.append(jnp.where(last_row, above[t], below[t]))
    for t in range(3):
        down_below, down_own = turned(below[t], -4), turned(beside[t], -4)
        main.append(jnp.where(last_row, down_below, down_own))
        extra.append(jnp.where(last_row, down_own, down_below))
    zero = jnp.zeros((ch, cols), F32)
    added = []
    for part in (main, extra):
        added.append([])
        for dy in range(3):
            mid = part[3 * dy + 1]
            added[-1] += [jnp.where(at_left, mid, 0.0), zero, jnp.where(at_left, 0.0, mid)]
    taps = [jnp.concatenate(part, axis=0).astype(BF16) for part in (main, extra, added[0], added[1])]
    edge = dot(conv_one_ref[...], jnp.concatenate(taps, axis=1))
    add_main, add_extra = edge[:, 2 * cols : 3 * cols], edge[:, 3 * cols :]
    edge = jnp.maximum(edge[:, : 2 * cols] + bias_one, 0.0)
    outside = jnp.logical_or(
        jnp.logical_and(at_left, c == 0), jnp.logical_and(jnp.logical_not(at_left), c == n_col - 1)
    )
    off_grid = jnp.logical_or(
        jnp.logical_and(last_row, r == 0), jnp.logical_and(jnp.logical_not(last_row), r == n_row - 1)
    )
    edge_main = jnp.where(outside, 0.0, edge[:, :cols])
    edge_extra = jnp.where(jnp.logical_or(outside, off_grid), 0.0, edge[:, cols:])

    ends = jnp.logical_or(lane == 0, lane == cols - 1)

    def put(pair, side, edges, adds, blank=None):
        base, out = pair * (6 * ch), pair * (2 * ch)
        if not isinstance(pair, int):
            base, out = pl.multiple_of(base, 6 * ch), pl.multiple_of(out, 2 * ch)
        where = slice(side * cols, (side + 1) * cols)
        for o in range(2):
            part = raw[pl.ds(out + o * ch, ch), where] + jnp.where(ends, adds[o], 0.0)
            part = jnp.maximum(part + bias_one, 0.0)
            if blank is not None and blank[0] == o:
                part = jnp.where(blank[1], 0.0, part)
            left = jnp.where(lane == 0, edges[o], pltpu.roll(part, 1, 1))
            right = jnp.where(lane == cols - 1, edges[o], pltpu.roll(part, cols - 1, 1))
            for t, piece in enumerate((left, part, right)):
                f3[pl.ds(base + (3 * o + t) * ch, ch), where] = piece.astype(BF16)

    def row_of_edge(x, h):
        return pltpu.roll(x, lax.rem(2 * cols - 4 * h, cols), 1)

    def both(h):
        return [(turned(x, -4 * h), turned(x, -4 * (h + 1))) for x in (edge_main, add_main)]

    def joined(first, h_first, second, h_second):
        return [
            (turned(a, -4 * h_first), turned(b, -4 * h_second)) for a, b in zip(first, second)
        ]

    inner, outer = (edge_main, add_main), (edge_extra, add_extra)
    put(0, 0, *joined(outer, rows - 1, inner, 0), blank=(0, r == 0))
    put(0, 1, *both(half - 1))

    def first_step(i, carry):
        for side in range(2):
            h = 2 * i - 1 + side * half
            put(i, side, *[(row_of_edge(x, h), row_of_edge(x, h + 1)) for x in inner])
        return carry

    lax.fori_loop(1, half // 2, first_step, 0)
    put(half // 2, 0, *both(half - 1))
    put(half // 2, 1, *joined(inner, rows - 1, outer, 0), blank=(1, r == n_row - 1))

    def second_step(j, acc):
        base = pl.multiple_of(j * (6 * ch), 6 * ch)
        return acc + jnp.maximum(dot(w2b[...], f3[pl.ds(base, 12 * ch), :]) + bias_two, 0.0)

    total = lax.fori_loop(0, half // 2, second_step, jnp.zeros((2 * ch, 2 * cols), F32))
    total = total[:ch] + total[ch:]
    total = total[:, :cols] + total[:, cols:]
    high = total.astype(BF16)
    low = (total - high.astype(F32)).astype(BF16)
    share = SLOT // local_count
    at = iota((SLOT, cols), 0) - local_count * lax.rem(me, share)
    pool = (iota((SLOT, cols), 1) // PATCH == at).astype(F32).astype(BF16)
    pooled = (dot_nt(pool, high) + dot_nt(pool, low)) * (1.0 / (PATCH * PATCH))
    shift = (iota((SLOT, local_count), 1) == at[:, :local_count]).astype(F32).astype(BF16)
    tokens = pooled + dot(shift, pos_ref[...])
    tokens = jnp.concatenate([tokens, jnp.zeros((SLOT, 128 - ch), F32)], axis=1).astype(BF16)
    token[...] = tokens
    gathered[pl.ds(pl.multiple_of(me * SLOT, SLOT), SLOT), :] = tokens

    def token_copy(i, j, sender):
        return pltpu.make_async_remote_copy(
            src_ref=token,
            dst_ref=gathered.at[pl.ds(pl.multiple_of(sender * SLOT, SLOT), SLOT)],
            send_sem=tok_send.at[i * n_col + j],
            recv_sem=tok_recv.at[sender],
            device_id=away(i, j),
            device_id_type=MESH,
        )

    def push(i, j, carry):
        token_copy(i, j, me).start()
        return carry

    def take(i, j, carry):
        token_copy(i, j, me).wait_send()
        rr, cc = away(i, j)
        token_copy(i, j, rr * n_col + cc).wait_recv()
        return carry

    others(push)
    others(take)

    every = gathered[...].astype(F32).reshape(n // share, share, SLOT, 128).sum(axis=1)
    every = every.reshape(n * local_count, 128).astype(BF16)[:, :ch]
    keys = dot(every, w_key_ref[...]).astype(BF16)
    values = dot(every, w_value_ref[...]).astype(BF16)
    score = dot_nt(heads, keys) * (1.0 / HEAD_DIM**0.5)
    peak = jnp.max(jnp.where(seen, score, -1e30), axis=1, keepdims=True)
    weight = jnp.where(seen, jnp.exp(score - peak), 0.0)
    norm = jnp.sum(weight, axis=1, keepdims=True)
    mixed = dot(weight.astype(BF16), values) / norm
    mixed = jnp.where(own_head, mixed, 0.0)
    attended = mixed[0:owned]
    for h in range(1, HEADS):
        attended = attended + mixed[h * owned : (h + 1) * owned]
    out_ref[...] = dot(attended.astype(BF16), w_out_ref[...]).astype(BF16)


def on_device(
    raster,
    conv_one,
    bias_one,
    conv_two,
    bias_two,
    pos_embed,
    query_embed,
    w_query,
    w_key,
    w_value,
    w_out,
    visible,
):
    ch, rows, cols = raster.shape
    n_row, n_col = lax.axis_size("row"), lax.axis_size("col")
    n = n_row * n_col
    owned = query_embed.shape[0] // n
    e = query_embed.shape[1]
    dma = pltpu.SemaphoreType.DMA
    operands = (
        raster,
        conv_one,
        bias_one.reshape(1, ch),
        conv_two,
        bias_two.reshape(1, ch),
        pos_embed.transpose(1, 2, 0).reshape(-1, ch),
        query_embed,
        w_query,
        w_key,
        w_value,
        w_out,
        visible,
    )
    operands = tuple(pltpu.with_memory_space_constraint(x, pltpu.HBM) for x in operands)
    wide = 3 * ch, 2 * cols
    return pl.pallas_call(
        functools.partial(kernel, (n_row, n_col, ch, rows, cols)),
        out_shape=jax.ShapeDtypeStruct((owned, e), BF16),
        in_specs=[pl.BlockSpec(memory_space=pltpu.HBM)] * len(operands),
        out_specs=pl.BlockSpec(memory_space=pltpu.VMEM),
        scratch_shapes=[pltpu.VMEM(x.shape, x.dtype) for x in operands]
        + [
            pltpu.VMEM((rows, ch, cols), BF16),
            pltpu.VMEM(((rows // 2 + 4) * wide[0], wide[1]), BF16),
            pltpu.VMEM(((rows // 4 + 1) * 2 * ch, 2 * cols), F32),
            pltpu.VMEM(((rows // 2 + 2) * wide[0], wide[1]), BF16),
            pltpu.VMEM((2 * ch, 12 * ch), BF16),
            pltpu.VMEM((2 * ch, 12 * ch), BF16),
            pltpu.VMEM((ch, cols), BF16),
            pltpu.VMEM((2, 2, ch, cols), BF16),
            pltpu.VMEM((8, ch, cols), BF16),
            pltpu.VMEM((SLOT, 128), BF16),
            pltpu.VMEM((n * SLOT, 128), BF16),
            dma((len(operands) + 3,)),
            dma((2,)),
            dma((2,)),
            dma((8,)),
            dma((8,)),
            dma((n,)),
            dma((n,)),
        ],
        compiler_params=pltpu.CompilerParams(
            collective_id=0, has_side_effects=True, vmem_limit_bytes=32 * 1024 * 1024
        ),
        cost_estimate=pl.CostEstimate(flops=1_000_000_000, bytes_accessed=2_000_000, transcendentals=0),
    )(*operands)


def solution(mesh):
    tile = P(None, "row", "col")
    in_specs = (tile, P(), P(), P(), P(), tile, P(), P(), P(), P(), P(), P())
    return jax.shard_map(
        on_device,
        mesh=mesh,
        in_specs=in_specs,
        out_specs=P(("row", "col"), None),
        check_vma=False,
    )
```

```python
import functools

import jax
import jax.numpy as jnp
from jax import lax
from jax.experimental import pallas as pl
from jax.experimental.pallas import tpu as pltpu
from jax.sharding import PartitionSpec as P

HEADS = 8
HEAD_DIM = 32
PATCH = 32
QBLOCK = 128
SLOT = 16
MESH = pl.DeviceIdType.MESH
F32 = jnp.float32
BF16 = jnp.bfloat16
SIDES = ((0, -1), (0, 1), (-1, 0), (1, 0), (-1, -1), (-1, 1), (1, -1), (1, 1))


def iota(shape, dim):
    return lax.broadcasted_iota(jnp.int32, shape, dim)


def dot(a, b):
    return jnp.dot(a, b, preferred_element_type=F32)


def dot_nt(a, b):
    return lax.dot_general(a, b, (((1,), (1,)), ((), ())), preferred_element_type=F32)


def column(row_vec):
    n = row_vec.shape[1]
    spread = jnp.where(iota((n, n), 0) == iota((n, n), 1), row_vec, 0.0)
    return jnp.sum(spread, axis=1, keepdims=True)


def kernel(sizes, *refs):
    n_row, n_col, ch, rows, cols = sizes
    operands, out_ref, local = refs[:12], refs[12], refs[13:25]
    (xt, x3, raw, f3, w2a, w2b, pack, rows_in, packs_in, token, by_row, block, gathered) = refs[25:38]
    (load_sem, row_send, row_recv, pack_send, pack_recv) = refs[38:43]
    (up_send, up_recv, side_send, side_recv) = refs[43:]
    (
        raster_ref,
        conv_one_ref,
        bias_one_ref,
        conv_two_ref,
        bias_two_ref,
        pos_ref,
        embed_ref,
        w_query_ref,
        w_key_ref,
        w_value_ref,
        w_out_ref,
        visible_ref,
    ) = local
    n = n_row * n_col
    r = lax.axis_index("row")
    c = lax.axis_index("col")
    me = r * n_col + c
    owned = out_ref.shape[0]
    e = out_ref.shape[1]
    half = rows // 2

    chunk = ch // 4
    raster_loads = [
        pltpu.make_async_copy(
            operands[0].at[pl.ds(i * chunk, chunk)], raster_ref.at[pl.ds(i * chunk, chunk)], load_sem.at[i]
        )
        for i in range(4)
    ]
    loads = [
        pltpu.make_async_copy(operands[i], local[i], load_sem.at[i + 3]) for i in range(1, len(operands))
    ]
    for copy in raster_loads:
        copy.start()

    def row_peer(i):
        rr = r + i
        return jnp.where(rr >= n_row, rr - n_row, rr)

    def col_peer(j):
        cc = c + j
        return jnp.where(cc >= n_col, cc - n_col, cc)

    def row_there(up):
        return r > 0 if up else r < n_row - 1

    def side_there(index):
        dr, dc = SIDES[index]
        ok = None
        if dr:
            ok = row_there(dr < 0)
        if dc:
            beside = c > 0 if dc < 0 else c < n_col - 1
            ok = beside if ok is None else jnp.logical_and(ok, beside)
        return ok

    barrier = pltpu.get_barrier_semaphore()

    def greet(device):
        pl.semaphore_signal(barrier, inc=1, device_id=device, device_id_type=MESH)

    lax.fori_loop(1, n_col, lambda j, carry: (greet((r, col_peer(j))), carry)[1], 0)
    lax.fori_loop(1, n_row, lambda i, carry: (greet((row_peer(i), c)), carry)[1], 0)
    corners = [index for index in range(8) if SIDES[index][0] and SIDES[index][1]]
    for index in corners:
        dr, dc = SIDES[index]
        pl.when(side_there(index))(lambda dr=dr, dc=dc: greet((r + dr, c + dc)))
    for copy in loads:
        copy.start()

    for i, copy in enumerate(raster_loads):
        copy.wait()
        part = raster_ref[i * chunk : (i + 1) * chunk].astype(F32)
        xt[:, i * chunk : (i + 1) * chunk, :] = jnp.transpose(part, (1, 0, 2)).astype(BF16)

    lane = iota((ch, cols), 1)
    group = lax.rem(lane + 2, cols) // 4

    def pack_rows(i, acc):
        for j in range(4):
            h = i * 4 + j
            acc = jnp.where(group == h, pltpu.roll(xt[h].astype(F32), h * 4, 1), acc)
        return acc

    packed = lax.fori_loop(0, rows // 4, pack_rows, jnp.zeros((ch, cols), F32))
    pack[...] = packed.astype(BF16)

    high_low = jnp.where(r > 0, 1, 0) + jnp.where(r < n_row - 1, 1, 0)
    left_right = jnp.where(c > 0, 1, 0) + jnp.where(c < n_col - 1, 1, 0)
    pl.semaphore_wait(barrier, n_row + n_col - 2 + high_low * left_right)

    def row_copy(up):
        return pltpu.make_async_remote_copy(
            src_ref=xt.at[pl.ds(0 if up else rows - 2, 2)],
            dst_ref=rows_in.at[1 if up else 0],
            send_sem=row_send.at[0 if up else 1],
            recv_sem=row_recv.at[1 if up else 0],
            device_id=(r - 1 if up else r + 1, c),
            device_id_type=MESH,
        )

    def pack_copy(index):
        dr, dc = SIDES[index]
        there = SIDES.index((-dr, -dc))
        return pltpu.make_async_remote_copy(
            src_ref=pack,
            dst_ref=packs_in.at[there],
            send_sem=pack_send.at[index],
            recv_sem=pack_recv.at[there],
            device_id=(r + dr, c + dc),
            device_id_type=MESH,
        )

    for up in (True, False):
        pl.when(row_there(up))(lambda up=up: row_copy(up).start())
    for index in range(8):
        pl.when(side_there(index))(lambda index=index: pack_copy(index).start())

    for copy in loads:
        copy.wait()

    for conv_ref, w2 in ((conv_one_ref, w2a), (conv_two_ref, w2b)):
        w = conv_ref[...]
        pad = jnp.zeros((ch, 3 * ch), BF16)
        w2[0:ch, :] = jnp.concatenate([w, pad], axis=1)
        w2[ch : 2 * ch, :] = jnp.concatenate([pad, w], axis=1)

    def fill(slot, side, center):
        left = jnp.where(lane == 0, 0.0, pltpu.roll(center, 1, 1))
        right = jnp.where(lane == cols - 1, 0.0, pltpu.roll(center, cols - 1, 1))
        base = slot * (3 * ch)
        if not isinstance(slot, int):
            base = pl.multiple_of(base, 3 * ch)
        where = slice(side * cols, (side + 1) * cols)
        for t, part in enumerate((left, center, right)):
            x3[pl.ds(base + t * ch, ch), where] = part.astype(BF16)

    def fill_rows(i, carry):
        for j in range(2):
            for side in range(2):
                s = i * 2 + j
                fill(s + 2 - 2 * side, side, xt[s + side * (half - 2)].astype(F32))
        return carry

    lax.fori_loop(0, half // 2 + 1, fill_rows, 0)

    def first_sums(i, carry):
        base = i * (6 * ch)
        out = i * (2 * ch)
        if not isinstance(i, int):
            base, out = pl.multiple_of(base, 6 * ch), pl.multiple_of(out, 2 * ch)
        raw[pl.ds(out, 2 * ch), :] = dot(w2a[...], x3[pl.ds(base, 12 * ch), :])
        return carry

    lax.fori_loop(1, half // 2, first_sums, 0)

    bias_one = column(bias_one_ref[...])
    bias_two = column(bias_two_ref[...])
    bias_two = jnp.concatenate([bias_two, bias_two], axis=0)

    for up in (True, False):

        @pl.when(row_there(up))
        def _(up=up):
            row_copy(up).wait_send()
            row_copy(not up).wait_recv()

        @pl.when(jnp.logical_not(row_there(up)))
        def _(up=up):
            rows_in[0 if up else 1] = jnp.zeros((2, ch, cols), BF16)

    for index in range(8):

        @pl.when(side_there(index))
        def _(index=index):
            back = SIDES.index((-SIDES[index][0], -SIDES[index][1]))
            pack_copy(index).wait_send()
            pack_copy(back).wait_recv()

        @pl.when(jnp.logical_not(side_there(index)))
        def _(index=index):
            packs_in[index] = jnp.zeros((ch, cols), BF16)

    at_left = lax.rem(lane, 4) == 0

    def turned(x, shift):
        return pltpu.roll(x, shift % cols, 1)

    def rim(dr):
        left = packs_in[SIDES.index((dr, -1))].astype(F32)
        right = packs_in[SIDES.index((dr, 1))].astype(F32)
        mid = packs_in[SIDES.index((dr, 0))].astype(F32) if dr else packed
        return (
            jnp.where(at_left, turned(left, 2), mid),
            jnp.where(at_left, turned(left, 1), turned(right, -1)),
            jnp.where(at_left, mid, turned(right, -2)),
        )

    above, beside, below = rim(-1), rim(0), rim(1)

    for j in range(2):
        fill(j, 0, rows_in[0, j].astype(F32))
        fill(half + 2 + j, 1, rows_in[1, j].astype(F32))
    first_sums(0, 0)
    first_sums(half // 2, 0)

    row_of = lax.rem(lane + 1, cols) // 4
    first_row, last_row = row_of == 0, row_of == rows - 1
    main, extra = [], []
    for t in range(3):
        up_above, up_own = turned(above[t], 4), turned(beside[t], 4)
        main.append(jnp.where(first_row, up_above, up_own))
        extra.append(jnp.where(last_row, up_above, up_own))
    for t in range(3):
        main.append(beside[t])
        extra.append(jnp.where(last_row, above[t], below[t]))
    for t in range(3):
        down_below, down_own = turned(below[t], -4), turned(beside[t], -4)
        main.append(jnp.where(last_row, down_below, down_own))
        extra.append(jnp.where(last_row, down_own, down_below))
    zero = jnp.zeros((ch, cols), F32)
    added = []
    for part in (main, extra):
        added.append([])
        for dy in range(3):
            mid = part[3 * dy + 1]
            added[-1] += [jnp.where(at_left, mid, 0.0), zero, jnp.where(at_left, 0.0, mid)]
    taps = [jnp.concatenate(part, axis=0).astype(BF16) for part in (main, extra, added[0], added[1])]
    edge = dot(conv_one_ref[...], jnp.concatenate(taps, axis=1))
    add_main, add_extra = edge[:, 2 * cols : 3 * cols], edge[:, 3 * cols :]
    edge = jnp.maximum(edge[:, : 2 * cols] + bias_one, 0.0)
    outside = jnp.logical_or(
        jnp.logical_and(at_left, c == 0), jnp.logical_and(jnp.logical_not(at_left), c == n_col - 1)
    )
    off_grid = jnp.logical_or(
        jnp.logical_and(last_row, r == 0), jnp.logical_and(jnp.logical_not(last_row), r == n_row - 1)
    )
    edge_main = jnp.where(outside, 0.0, edge[:, :cols])
    edge_extra = jnp.where(jnp.logical_or(outside, off_grid), 0.0, edge[:, cols:])

    ends = jnp.logical_or(lane == 0, lane == cols - 1)

    def put(pair, side, edges, adds, blank=None):
        base, out = pair * (6 * ch), pair * (2 * ch)
        if not isinstance(pair, int):
            base, out = pl.multiple_of(base, 6 * ch), pl.multiple_of(out, 2 * ch)
        where = slice(side * cols, (side + 1) * cols)
        for o in range(2):
            part = raw[pl.ds(out + o * ch, ch), where] + jnp.where(ends, adds[o], 0.0)
            part = jnp.maximum(part + bias_one, 0.0)
            if blank is not None and blank[0] == o:
                part = jnp.where(blank[1], 0.0, part)
            left = jnp.where(lane == 0, edges[o], pltpu.roll(part, 1, 1))
            right = jnp.where(lane == cols - 1, edges[o], pltpu.roll(part, cols - 1, 1))
            for t, piece in enumerate((left, part, right)):
                f3[pl.ds(base + (3 * o + t) * ch, ch), where] = piece.astype(BF16)

    def row_of_edge(x, h):
        return pltpu.roll(x, lax.rem(2 * cols - 4 * h, cols), 1)

    def both(h):
        return [(turned(x, -4 * h), turned(x, -4 * (h + 1))) for x in (edge_main, add_main)]

    def joined(first, h_first, second, h_second):
        return [
            (turned(a, -4 * h_first), turned(b, -4 * h_second)) for a, b in zip(first, second)
        ]

    inner, outer = (edge_main, add_main), (edge_extra, add_extra)
    put(0, 0, *joined(outer, rows - 1, inner, 0), blank=(0, r == 0))
    put(0, 1, *both(half - 1))

    def first_step(i, carry):
        for side in range(2):
            h = 2 * i - 1 + side * half
            put(i, side, *[(row_of_edge(x, h), row_of_edge(x, h + 1)) for x in inner])
        return carry

    lax.fori_loop(1, half // 2, first_step, 0)
    put(half // 2, 0, *both(half - 1))
    put(half // 2, 1, *joined(inner, rows - 1, outer, 0), blank=(1, r == n_row - 1))

    def second_step(j, acc):
        base = pl.multiple_of(j * (6 * ch), 6 * ch)
        return acc + jnp.maximum(dot(w2b[...], f3[pl.ds(base, 12 * ch), :]) + bias_two, 0.0)

    total = lax.fori_loop(0, half // 2, second_step, jnp.zeros((2 * ch, 2 * cols), F32))
    total = total[:ch] + total[ch:]
    total = total[:, :cols] + total[:, cols:]
    high = total.astype(BF16)
    low = (total - high.astype(F32)).astype(BF16)
    local_count = pos_ref.shape[0]
    share = SLOT // local_count
    at = iota((SLOT, cols), 0) - local_count * lax.rem(r, share)
    pool = (iota((SLOT, cols), 1) // PATCH == at).astype(F32).astype(BF16)
    pooled = (dot_nt(pool, high) + dot_nt(pool, low)) * (1.0 / (PATCH * PATCH))
    shift = (iota((SLOT, local_count), 1) == at[:, :local_count]).astype(F32).astype(BF16)
    tokens = pooled + dot(shift, pos_ref[...])
    tokens = jnp.concatenate([tokens, jnp.zeros((SLOT, 128 - ch), F32)], axis=1).astype(BF16)
    token[...] = tokens
    by_row[pl.ds(pl.multiple_of(r * SLOT, SLOT), SLOT), :] = tokens

    def up_copy(i, sender):
        return pltpu.make_async_remote_copy(
            src_ref=token,
            dst_ref=by_row.at[pl.ds(pl.multiple_of(sender * SLOT, SLOT), SLOT)],
            send_sem=up_send.at[i],
            recv_sem=up_recv.at[sender],
            device_id=(row_peer(i), c),
            device_id_type=MESH,
        )

    depth = n_row * local_count

    def side_copy(j, sender):
        return pltpu.make_async_remote_copy(
            src_ref=block,
            dst_ref=gathered.at[pl.ds(pl.multiple_of(sender * depth, depth), depth)],
            send_sem=side_send.at[j],
            recv_sem=side_recv.at[sender],
            device_id=(r, col_peer(j)),
            device_id_type=MESH,
        )

    lax.fori_loop(1, n_row, lambda i, carry: (up_copy(i, r).start(), carry)[1], 0)

    pick = iota((owned, embed_ref.shape[0]), 1) == me * owned + iota((owned, embed_ref.shape[0]), 0)
    own = dot(pick.astype(F32).astype(BF16), embed_ref[...]).astype(BF16)
    query = dot(own, w_query_ref[...]).astype(BF16).astype(F32)
    tall = (HEADS * owned, e)
    own_head = iota(tall, 0) // owned == iota(tall, 1) // HEAD_DIM
    heads = jnp.where(own_head, jnp.concatenate([query] * HEADS, axis=0), 0.0).astype(BF16)
    def take_up(i, carry):
        up_copy(i, row_peer(i)).wait_recv()
        return carry

    lax.fori_loop(1, n_row, take_up, 0)
    dense = by_row[...].astype(F32).reshape(n_row // share, share, SLOT, 128).sum(axis=1)
    dense = dense.reshape(depth, 128).astype(BF16)
    block[...] = dense
    lax.fori_loop(1, n_col, lambda j, carry: (side_copy(j, c).start(), carry)[1], 0)
    gathered[pl.ds(pl.multiple_of(c * depth, depth), depth), :] = dense

    wide = (visible_ref.shape[1], n * local_count)
    spot = iota(wide, 1) // local_count
    tile = lax.rem(spot, n_row) * n_col + spot // n_row
    spread = tile == iota(wide, 0)
    blocks = visible_ref.shape
    mine = iota(blocks, 0) == me * owned // QBLOCK
    seen_row = jnp.sum(jnp.where(mine, visible_ref[...], 0).astype(F32), axis=0, keepdims=True)
    seen = dot(
        jnp.broadcast_to(seen_row, (8, blocks[1])).astype(BF16), spread.astype(F32).astype(BF16)
    )[0:1] > 0.5

    def wait_up(i, carry):
        up_copy(i, r).wait_send()
        return carry

    def take_side(j, carry):
        side_copy(j, c).wait_send()
        side_copy(j, col_peer(j)).wait_recv()
        return carry

    lax.fori_loop(1, n_row, wait_up, 0)
    lax.fori_loop(1, n_col, take_side, 0)

    every = gathered[...][:, :ch]
    keys = dot(every, w_key_ref[...]).astype(BF16)
    values = dot(every, w_value_ref[...]).astype(BF16)
    score = dot_nt(heads, keys) * (1.0 / HEAD_DIM**0.5)
    peak = jnp.max(jnp.where(seen, score, -1e30), axis=1, keepdims=True)
    weight = jnp.where(seen, jnp.exp(score - peak), 0.0)
    norm = jnp.sum(weight, axis=1, keepdims=True)
    mixed = dot(weight.astype(BF16), values) / norm
    mixed = jnp.where(own_head, mixed, 0.0)
    attended = mixed[0:owned]
    for h in range(1, HEADS):
        attended = attended + mixed[h * owned : (h + 1) * owned]
    out_ref[...] = dot(attended.astype(BF16), w_out_ref[...]).astype(BF16)


def on_device(
    raster,
    conv_one,
    bias_one,
    conv_two,
    bias_two,
    pos_embed,
    query_embed,
    w_query,
    w_key,
    w_value,
    w_out,
    visible,
):
    ch, rows, cols = raster.shape
    n_row, n_col = lax.axis_size("row"), lax.axis_size("col")
    n = n_row * n_col
    owned = query_embed.shape[0] // n
    e = query_embed.shape[1]
    local_count = pos_embed.shape[1] * pos_embed.shape[2]
    dma = pltpu.SemaphoreType.DMA
    operands = (
        raster,
        conv_one,
        bias_one.reshape(1, ch),
        conv_two,
        bias_two.reshape(1, ch),
        pos_embed.transpose(1, 2, 0).reshape(-1, ch),
        query_embed,
        w_query,
        w_key,
        w_value,
        w_out,
        visible,
    )
    operands = tuple(pltpu.with_memory_space_constraint(x, pltpu.HBM) for x in operands)
    wide = 3 * ch, 2 * cols
    return pl.pallas_call(
        functools.partial(kernel, (n_row, n_col, ch, rows, cols)),
        out_shape=jax.ShapeDtypeStruct((owned, e), BF16),
        in_specs=[pl.BlockSpec(memory_space=pltpu.HBM)] * len(operands),
        out_specs=pl.BlockSpec(memory_space=pltpu.VMEM),
        scratch_shapes=[pltpu.VMEM(x.shape, x.dtype) for x in operands]
        + [
            pltpu.VMEM((rows, ch, cols), BF16),
            pltpu.VMEM(((rows // 2 + 4) * wide[0], wide[1]), BF16),
            pltpu.VMEM(((rows // 4 + 1) * 2 * ch, 2 * cols), F32),
            pltpu.VMEM(((rows // 2 + 2) * wide[0], wide[1]), BF16),
            pltpu.VMEM((2 * ch, 12 * ch), BF16),
            pltpu.VMEM((2 * ch, 12 * ch), BF16),
            pltpu.VMEM((ch, cols), BF16),
            pltpu.VMEM((2, 2, ch, cols), BF16),
            pltpu.VMEM((8, ch, cols), BF16),
            pltpu.VMEM((SLOT, 128), BF16),
            pltpu.VMEM((n_row * SLOT, 128), BF16),
            pltpu.VMEM((n_row * local_count, 128), BF16),
            pltpu.VMEM((n * local_count, 128), BF16),
            dma((len(operands) + 3,)),
            dma((2,)),
            dma((2,)),
            dma((8,)),
            dma((8,)),
            dma((n_row,)),
            dma((n_row,)),
            dma((n_col,)),
            dma((n_col,)),
        ],
        compiler_params=pltpu.CompilerParams(
            collective_id=0, has_side_effects=True, vmem_limit_bytes=32 * 1024 * 1024
        ),
        cost_estimate=pl.CostEstimate(flops=1_000_000_000, bytes_accessed=2_000_000, transcendentals=0),
    )(*operands)


def solution(mesh):
    tile = P(None, "row", "col")
    in_specs = (tile, P(), P(), P(), P(), tile, P(), P(), P(), P(), P(), P())
    return jax.shard_map(
        on_device,
        mesh=mesh,
        in_specs=in_specs,
        out_specs=P(("row", "col"), None),
        check_vma=False,
    )
```

```python
import functools

import jax
import jax.numpy as jnp
from jax import lax
from jax.experimental import pallas as pl
from jax.experimental.pallas import tpu as pltpu
from jax.sharding import PartitionSpec as P

HEADS = 8
HEAD_DIM = 32
PATCH = 32
QBLOCK = 128
SLOT = 16
MESH = pl.DeviceIdType.MESH
F32 = jnp.float32
BF16 = jnp.bfloat16
SIDES = ((0, -1), (0, 1), (-1, 0), (1, 0), (-1, -1), (-1, 1), (1, -1), (1, 1))


def iota(shape, dim):
    return lax.broadcasted_iota(jnp.int32, shape, dim)


def dot(a, b):
    return jnp.dot(a, b, preferred_element_type=F32)


def dot_nt(a, b):
    return lax.dot_general(a, b, (((1,), (1,)), ((), ())), preferred_element_type=F32)


def column(row_vec):
    n = row_vec.shape[1]
    spread = jnp.where(iota((n, n), 0) == iota((n, n), 1), row_vec, 0.0)
    return jnp.sum(spread, axis=1, keepdims=True)


def kernel(sizes, *refs):
    n_row, n_col, ch, rows, cols = sizes
    operands, out_ref, local = refs[:12], refs[12], refs[13:25]
    (xt, x3, raw, f3, w2a, w2b, pack, rows_in, packs_in, token, gathered) = refs[25:36]
    (load_sem, row_send, row_recv, pack_send, pack_recv, tok_send, tok_recv) = refs[36:]
    (
        raster_ref,
        conv_one_ref,
        bias_one_ref,
        conv_two_ref,
        bias_two_ref,
        pos_ref,
        embed_ref,
        w_query_ref,
        w_key_ref,
        w_value_ref,
        w_out_ref,
        visible_ref,
    ) = local
    n = n_row * n_col
    r = lax.axis_index("row")
    c = lax.axis_index("col")
    me = r * n_col + c
    owned = out_ref.shape[0]
    e = out_ref.shape[1]
    half = rows // 2

    chunk = ch // 4
    raster_loads = [
        pltpu.make_async_copy(
            operands[0].at[pl.ds(i * chunk, chunk)], raster_ref.at[pl.ds(i * chunk, chunk)], load_sem.at[i]
        )
        for i in range(4)
    ]
    loads = [
        pltpu.make_async_copy(operands[i], local[i], load_sem.at[i + 3]) for i in range(1, len(operands))
    ]
    for copy in raster_loads:
        copy.start()

    def away(i, j):
        rr, cc = r + i, c + j
        return (jnp.where(rr >= n_row, rr - n_row, rr), jnp.where(cc >= n_col, cc - n_col, cc))

    def others(body):
        for i in range(n_row):
            lax.fori_loop(0 if i else 1, n_col, lambda j, carry, i=i: body(i, j, carry), 0)

    barrier = pltpu.get_barrier_semaphore()

    def greet(i, j, carry):
        pl.semaphore_signal(barrier, inc=1, device_id=away(i, j), device_id_type=MESH)
        return carry

    others(greet)
    for copy in loads:
        copy.start()

    for i, copy in enumerate(raster_loads):
        copy.wait()
        part = raster_ref[i * chunk : (i + 1) * chunk].astype(F32)
        xt[:, i * chunk : (i + 1) * chunk, :] = jnp.transpose(part, (1, 0, 2)).astype(BF16)

    lane = iota((ch, cols), 1)
    group = lax.rem(lane + 2, cols) // 4

    def pack_rows(i, acc):
        for j in range(4):
            h = i * 4 + j
            acc = jnp.where(group == h, pltpu.roll(xt[h].astype(F32), h * 4, 1), acc)
        return acc

    packed = lax.fori_loop(0, rows // 4, pack_rows, jnp.zeros((ch, cols), F32))
    pack[...] = packed.astype(BF16)

    pl.semaphore_wait(barrier, n - 1)

    def row_copy(up):
        return pltpu.make_async_remote_copy(
            src_ref=xt.at[pl.ds(0 if up else rows - 2, 2)],
            dst_ref=rows_in.at[1 if up else 0],
            send_sem=row_send.at[0 if up else 1],
            recv_sem=row_recv.at[1 if up else 0],
            device_id=(r - 1 if up else r + 1, c),
            device_id_type=MESH,
        )

    def pack_copy(index):
        dr, dc = SIDES[index]
        there = SIDES.index((-dr, -dc))
        return pltpu.make_async_remote_copy(
            src_ref=pack,
            dst_ref=packs_in.at[there],
            send_sem=pack_send.at[index],
            recv_sem=pack_recv.at[there],
            device_id=(r + dr, c + dc),
            device_id_type=MESH,
        )

    def row_there(up):
        return r > 0 if up else r < n_row - 1

    def side_there(index):
        dr, dc = SIDES[index]
        ok = None
        if dr:
            ok = row_there(dr < 0)
        if dc:
            beside = c > 0 if dc < 0 else c < n_col - 1
            ok = beside if ok is None else jnp.logical_and(ok, beside)
        return ok

    for up in (True, False):
        pl.when(row_there(up))(lambda up=up: row_copy(up).start())
    for index in range(8):
        pl.when(side_there(index))(lambda index=index: pack_copy(index).start())

    for copy in loads:
        copy.wait()

    for conv_ref, w2 in ((conv_one_ref, w2a), (conv_two_ref, w2b)):
        w = conv_ref[...]
        pad = jnp.zeros((ch, 3 * ch), BF16)
        w2[0:ch, :] = jnp.concatenate([w, pad], axis=1)
        w2[ch : 2 * ch, :] = jnp.concatenate([pad, w], axis=1)

    def fill(slot, side, center):
        left = jnp.where(lane == 0, 0.0, pltpu.roll(center, 1, 1))
        right = jnp.where(lane == cols - 1, 0.0, pltpu.roll(center, cols - 1, 1))
        base = slot * (3 * ch)
        if not isinstance(slot, int):
            base = pl.multiple_of(base, 3 * ch)
        where = slice(side * cols, (side + 1) * cols)
        for t, part in enumerate((left, center, right)):
            x3[pl.ds(base + t * ch, ch), where] = part.astype(BF16)

    def fill_rows(i, carry):
        for j in range(2):
            for side in range(2):
                s = i * 2 + j
                fill(s + 2 - 2 * side, side, xt[s + side * (half - 2)].astype(F32))
        return carry

    lax.fori_loop(0, half // 2 + 1, fill_rows, 0)

    def first_sums(i, carry):
        base = i * (6 * ch)
        out = i * (2 * ch)
        if not isinstance(i, int):
            base, out = pl.multiple_of(base, 6 * ch), pl.multiple_of(out, 2 * ch)
        raw[pl.ds(out, 2 * ch), :] = dot(w2a[...], x3[pl.ds(base, 12 * ch), :])
        return carry

    for i in range(1, half // 2):
        first_sums(i, 0)

    bias_one = column(bias_one_ref[...])
    bias_two = column(bias_two_ref[...])
    bias_two = jnp.concatenate([bias_two, bias_two], axis=0)

    for up in (True, False):

        @pl.when(row_there(up))
        def _(up=up):
            row_copy(up).wait_send()
            row_copy(not up).wait_recv()

        @pl.when(jnp.logical_not(row_there(up)))
        def _(up=up):
            rows_in[0 if up else 1] = jnp.zeros((2, ch, cols), BF16)

    for index in range(8):

        @pl.when(side_there(index))
        def _(index=index):
            back = SIDES.index((-SIDES[index][0], -SIDES[index][1]))
            pack_copy(index).wait_send()
            pack_copy(back).wait_recv()

        @pl.when(jnp.logical_not(side_there(index)))
        def _(index=index):
            packs_in[index] = jnp.zeros((ch, cols), BF16)

    at_left = lax.rem(lane, 4) == 0

    def turned(x, shift):
        return pltpu.roll(x, shift % cols, 1)

    def rim(dr):
        left = packs_in[SIDES.index((dr, -1))].astype(F32)
        right = packs_in[SIDES.index((dr, 1))].astype(F32)
        mid = packs_in[SIDES.index((dr, 0))].astype(F32) if dr else packed
        return (
            jnp.where(at_left, turned(left, 2), mid),
            jnp.where(at_left, turned(left, 1), turned(right, -1)),
            jnp.where(at_left, mid, turned(right, -2)),
        )

    above, beside, below = rim(-1), rim(0), rim(1)

    for j in range(2):
        fill(j, 0, rows_in[0, j].astype(F32))
        fill(half + 2 + j, 1, rows_in[1, j].astype(F32))
    first_sums(0, 0)
    first_sums(half // 2, 0)

    row_of = lax.rem(lane + 1, cols) // 4
    first_row, last_row = row_of == 0, row_of == rows - 1
    main, extra = [], []
    for t in range(3):
        up_above, up_own = turned(above[t], 4), turned(beside[t], 4)
        main.append(jnp.where(first_row, up_above, up_own))
        extra.append(jnp.where(last_row, up_above, up_own))
    for t in range(3):
        main.append(beside[t])
        extra.append(jnp.where(last_row, above[t], below[t]))
    for t in range(3):
        down_below, down_own = turned(below[t], -4), turned(beside[t], -4)
        main.append(jnp.where(last_row, down_below, down_own))
        extra.append(jnp.where(last_row, down_own, down_below))
    zero = jnp.zeros((ch, cols), F32)
    added = []
    for part in (main, extra):
        added.append([])
        for dy in range(3):
            mid = part[3 * dy + 1]
            added[-1] += [jnp.where(at_left, mid, 0.0), zero, jnp.where(at_left, 0.0, mid)]
    taps = [jnp.concatenate(part, axis=0).astype(BF16) for part in (main, extra, added[0], added[1])]
    edge = dot(conv_one_ref[...], jnp.concatenate(taps, axis=1))
    add_main, add_extra = edge[:, 2 * cols : 3 * cols], edge[:, 3 * cols :]
    edge = jnp.maximum(edge[:, : 2 * cols] + bias_one, 0.0)
    outside = jnp.logical_or(
        jnp.logical_and(at_left, c == 0), jnp.logical_and(jnp.logical_not(at_left), c == n_col - 1)
    )
    off_grid = jnp.logical_or(
        jnp.logical_and(last_row, r == 0), jnp.logical_and(jnp.logical_not(last_row), r == n_row - 1)
    )
    edge_main = jnp.where(outside, 0.0, edge[:, :cols])
    edge_extra = jnp.where(jnp.logical_or(outside, off_grid), 0.0, edge[:, cols:])

    ends = jnp.logical_or(lane == 0, lane == cols - 1)

    def put(pair, side, edges, adds, blank=None):
        base, out = pair * (6 * ch), pair * (2 * ch)
        if not isinstance(pair, int):
            base, out = pl.multiple_of(base, 6 * ch), pl.multiple_of(out, 2 * ch)
        where = slice(side * cols, (side + 1) * cols)
        for o in range(2):
            part = raw[pl.ds(out + o * ch, ch), where] + jnp.where(ends, adds[o], 0.0)
            part = jnp.maximum(part + bias_one, 0.0)
            if blank is not None and blank[0] == o:
                part = jnp.where(blank[1], 0.0, part)
            left = jnp.where(lane == 0, edges[o], pltpu.roll(part, 1, 1))
            right = jnp.where(lane == cols - 1, edges[o], pltpu.roll(part, cols - 1, 1))
            for t, piece in enumerate((left, part, right)):
                f3[pl.ds(base + (3 * o + t) * ch, ch), where] = piece.astype(BF16)

    def row_of_edge(x, h):
        return pltpu.roll(x, lax.rem(2 * cols - 4 * h, cols), 1)

    def both(h):
        return [(turned(x, -4 * h), turned(x, -4 * (h + 1))) for x in (edge_main, add_main)]

    def joined(first, h_first, second, h_second):
        return [
            (turned(a, -4 * h_first), turned(b, -4 * h_second)) for a, b in zip(first, second)
        ]

    inner, outer = (edge_main, add_main), (edge_extra, add_extra)
    put(0, 0, *joined(outer, rows - 1, inner, 0), blank=(0, r == 0))
    put(0, 1, *both(half - 1))

    def first_step(i, carry):
        for side in range(2):
            h = 2 * i - 1 + side * half
            put(i, side, *[(row_of_edge(x, h), row_of_edge(x, h + 1)) for x in inner])
        return carry

    lax.fori_loop(1, half // 2, first_step, 0)
    put(half // 2, 0, *both(half - 1))
    put(half // 2, 1, *joined(inner, rows - 1, outer, 0), blank=(1, r == n_row - 1))

    total = jnp.zeros((2 * ch, 2 * cols), F32)
    for j in range(half // 2):
        part = dot(w2b[...], f3[j * (6 * ch) : (j + 2) * (6 * ch), :])
        total = total + jnp.maximum(part + bias_two, 0.0)
    total = total[:ch] + total[ch:]
    total = total[:, :cols] + total[:, cols:]
    high = total.astype(BF16)
    low = (total - high.astype(F32)).astype(BF16)
    local_count = pos_ref.shape[0]
    share = SLOT // local_count
    at = iota((SLOT, cols), 0) - local_count * lax.rem(me, share)
    pool = (iota((SLOT, cols), 1) // PATCH == at).astype(F32).astype(BF16)
    pooled = (dot_nt(pool, high) + dot_nt(pool, low)) * (1.0 / (PATCH * PATCH))
    shift = (iota((SLOT, local_count), 1) == at[:, :local_count]).astype(F32).astype(BF16)
    tokens = pooled + dot(shift, pos_ref[...])
    tokens = jnp.concatenate([tokens, jnp.zeros((SLOT, 128 - ch), F32)], axis=1).astype(BF16)
    token[...] = tokens
    gathered[pl.ds(pl.multiple_of(me * SLOT, SLOT), SLOT), :] = tokens

    def token_copy(i, j, sender):
        return pltpu.make_async_remote_copy(
            src_ref=token,
            dst_ref=gathered.at[pl.ds(pl.multiple_of(sender * SLOT, SLOT), SLOT)],
            send_sem=tok_send.at[i * n_col + j],
            recv_sem=tok_recv.at[sender],
            device_id=away(i, j),
            device_id_type=MESH,
        )

    def push(i, j, carry):
        token_copy(i, j, me).start()
        return carry

    def take(i, j, carry):
        token_copy(i, j, me).wait_send()
        rr, cc = away(i, j)
        token_copy(i, j, rr * n_col + cc).wait_recv()
        return carry

    others(push)

    pick = iota((owned, embed_ref.shape[0]), 1) == me * owned + iota((owned, embed_ref.shape[0]), 0)
    own = dot(pick.astype(F32).astype(BF16), embed_ref[...]).astype(BF16)
    query = dot(own, w_query_ref[...]).astype(BF16).astype(F32)
    tall = (HEADS * owned, e)
    own_head = iota(tall, 0) // owned == iota(tall, 1) // HEAD_DIM
    heads = jnp.where(own_head, jnp.concatenate([query] * HEADS, axis=0), 0.0).astype(BF16)
    wide = (visible_ref.shape[1], n * local_count)
    spread = iota(wide, 1) // local_count == iota(wide, 0)
    blocks = visible_ref.shape
    mine = iota(blocks, 0) == me * owned // QBLOCK
    seen_row = jnp.sum(jnp.where(mine, visible_ref[...], 0).astype(F32), axis=0, keepdims=True)
    seen = dot(
        jnp.broadcast_to(seen_row, (8, blocks[1])).astype(BF16), spread.astype(F32).astype(BF16)
    )[0:1] > 0.5

    others(take)

    every = gathered[...].astype(F32).reshape(n // share, share, SLOT, 128).sum(axis=1)
    every = every.reshape(n * local_count, 128).astype(BF16)[:, :ch]
    keys = dot(every, w_key_ref[...]).astype(BF16)
    values = dot(every, w_value_ref[...]).astype(BF16)
    score = dot_nt(heads, keys) * (1.0 / HEAD_DIM**0.5)
    peak = jnp.max(jnp.where(seen, score, -1e30), axis=1, keepdims=True)
    weight = jnp.where(seen, jnp.exp(score - peak), 0.0)
    norm = jnp.sum(weight, axis=1, keepdims=True)
    mixed = dot(weight.astype(BF16), values) / norm
    mixed = jnp.where(own_head, mixed, 0.0)
    attended = mixed[0:owned]
    for h in range(1, HEADS):
        attended = attended + mixed[h * owned : (h + 1) * owned]
    out_ref[...] = dot(attended.astype(BF16), w_out_ref[...]).astype(BF16)


def on_device(
    raster,
    conv_one,
    bias_one,
    conv_two,
    bias_two,
    pos_embed,
    query_embed,
    w_query,
    w_key,
    w_value,
    w_out,
    visible,
):
    ch, rows, cols = raster.shape
    n_row, n_col = lax.axis_size("row"), lax.axis_size("col")
    n = n_row * n_col
    owned = query_embed.shape[0] // n
    e = query_embed.shape[1]
    dma = pltpu.SemaphoreType.DMA
    operands = (
        raster,
        conv_one,
        bias_one.reshape(1, ch),
        conv_two,
        bias_two.reshape(1, ch),
        pos_embed.transpose(1, 2, 0).reshape(-1, ch),
        query_embed,
        w_query,
        w_key,
        w_value,
        w_out,
        visible,
    )
    operands = tuple(pltpu.with_memory_space_constraint(x, pltpu.HBM) for x in operands)
    wide = 3 * ch, 2 * cols
    return pl.pallas_call(
        functools.partial(kernel, (n_row, n_col, ch, rows, cols)),
        out_shape=jax.ShapeDtypeStruct((owned, e), BF16),
        in_specs=[pl.BlockSpec(memory_space=pltpu.HBM)] * len(operands),
        out_specs=pl.BlockSpec(memory_space=pltpu.VMEM),
        scratch_shapes=[pltpu.VMEM(x.shape, x.dtype) for x in operands]
        + [
            pltpu.VMEM((rows, ch, cols), BF16),
            pltpu.VMEM(((rows // 2 + 4) * wide[0], wide[1]), BF16),
            pltpu.VMEM(((rows // 4 + 1) * 2 * ch, 2 * cols), F32),
            pltpu.VMEM(((rows // 2 + 2) * wide[0], wide[1]), BF16),
            pltpu.VMEM((2 * ch, 12 * ch), BF16),
            pltpu.VMEM((2 * ch, 12 * ch), BF16),
            pltpu.VMEM((ch, cols), BF16),
            pltpu.VMEM((2, 2, ch, cols), BF16),
            pltpu.VMEM((8, ch, cols), BF16),
            pltpu.VMEM((SLOT, 128), BF16),
            pltpu.VMEM((n * SLOT, 128), BF16),
            dma((len(operands) + 3,)),
            dma((2,)),
            dma((2,)),
            dma((8,)),
            dma((8,)),
            dma((n,)),
            dma((n,)),
        ],
        compiler_params=pltpu.CompilerParams(
            collective_id=0, has_side_effects=True, vmem_limit_bytes=32 * 1024 * 1024
        ),
        cost_estimate=pl.CostEstimate(flops=1_000_000_000, bytes_accessed=2_000_000, transcendentals=0),
    )(*operands)


def solution(mesh):
    tile = P(None, "row", "col")
    in_specs = (tile, P(), P(), P(), P(), tile, P(), P(), P(), P(), P(), P())
    return jax.shard_map(
        on_device,
        mesh=mesh,
        in_specs=in_specs,
        out_specs=P(("row", "col"), None),
        check_vma=False,
    )
```

```python
import functools

import jax
import jax.numpy as jnp
from jax import lax
from jax.experimental import pallas as pl
from jax.experimental.pallas import tpu as pltpu
from jax.sharding import PartitionSpec as P

HEADS = 8
HEAD_DIM = 32
PATCH = 32
QBLOCK = 128
SLOT = 16
MESH = pl.DeviceIdType.MESH
F32 = jnp.float32
BF16 = jnp.bfloat16
SIDES = ((0, -1), (0, 1), (-1, 0), (1, 0), (-1, -1), (-1, 1), (1, -1), (1, 1))


def iota(shape, dim):
    return lax.broadcasted_iota(jnp.int32, shape, dim)


def dot(a, b):
    return jnp.dot(a, b, preferred_element_type=F32)


def dot_nt(a, b):
    return lax.dot_general(a, b, (((1,), (1,)), ((), ())), preferred_element_type=F32)


def column(row_vec):
    n = row_vec.shape[1]
    spread = jnp.where(iota((n, n), 0) == iota((n, n), 1), row_vec, 0.0)
    return jnp.sum(spread, axis=1, keepdims=True)


def kernel(sizes, *refs):
    n_row, n_col, ch, rows, cols = sizes
    operands, out_ref, local = refs[:12], refs[12], refs[13:25]
    (xt, x3, raw, f3, w2a, w2b, pack, rows_in, packs_in, token, gathered) = refs[25:36]
    (load_sem, row_send, row_recv, pack_send, pack_recv, tok_send, tok_recv) = refs[36:]
    (
        raster_ref,
        conv_one_ref,
        bias_one_ref,
        conv_two_ref,
        bias_two_ref,
        pos_ref,
        embed_ref,
        w_query_ref,
        w_key_ref,
        w_value_ref,
        w_out_ref,
        visible_ref,
    ) = local
    n = n_row * n_col
    r = lax.axis_index("row")
    c = lax.axis_index("col")
    me = r * n_col + c
    owned = out_ref.shape[0]
    e = out_ref.shape[1]
    half = rows // 2

    chunk = ch // 4
    raster_loads = [
        pltpu.make_async_copy(
            operands[0].at[pl.ds(i * chunk, chunk)], raster_ref.at[pl.ds(i * chunk, chunk)], load_sem.at[i]
        )
        for i in range(4)
    ]
    loads = [
        pltpu.make_async_copy(operands[i], local[i], load_sem.at[i + 3]) for i in range(1, len(operands))
    ]
    for copy in raster_loads:
        copy.start()

    def away(i, j):
        rr, cc = r + i, c + j
        return (jnp.where(rr >= n_row, rr - n_row, rr), jnp.where(cc >= n_col, cc - n_col, cc))

    def others(body):
        for i in range(n_row):
            lax.fori_loop(0 if i else 1, n_col, lambda j, carry, i=i: body(i, j, carry), 0)

    barrier = pltpu.get_barrier_semaphore()

    def greet(i, j, carry):
        pl.semaphore_signal(barrier, inc=1, device_id=away(i, j), device_id_type=MESH)
        return carry

    others(greet)
    for copy in loads:
        copy.start()

    for i, copy in enumerate(raster_loads):
        copy.wait()
        part = raster_ref[i * chunk : (i + 1) * chunk].astype(F32)
        xt[:, i * chunk : (i + 1) * chunk, :] = jnp.transpose(part, (1, 0, 2)).astype(BF16)

    lane = iota((ch, cols), 1)
    group = lax.rem(lane + 2, cols) // 4

    def pack_rows(i, acc):
        for j in range(4):
            h = i * 4 + j
            acc = jnp.where(group == h, pltpu.roll(xt[h].astype(F32), h * 4, 1), acc)
        return acc

    packed = lax.fori_loop(0, rows // 4, pack_rows, jnp.zeros((ch, cols), F32))
    pack[...] = packed.astype(BF16)

    pl.semaphore_wait(barrier, n - 1)

    def row_copy(up):
        return pltpu.make_async_remote_copy(
            src_ref=xt.at[pl.ds(0 if up else rows - 2, 2)],
            dst_ref=rows_in.at[1 if up else 0],
            send_sem=row_send.at[0 if up else 1],
            recv_sem=row_recv.at[1 if up else 0],
            device_id=(r - 1 if up else r + 1, c),
            device_id_type=MESH,
        )

    def pack_copy(index):
        dr, dc = SIDES[index]
        there = SIDES.index((-dr, -dc))
        return pltpu.make_async_remote_copy(
            src_ref=pack,
            dst_ref=packs_in.at[there],
            send_sem=pack_send.at[index],
            recv_sem=pack_recv.at[there],
            device_id=(r + dr, c + dc),
            device_id_type=MESH,
        )

    def row_there(up):
        return r > 0 if up else r < n_row - 1

    def side_there(index):
        dr, dc = SIDES[index]
        ok = None
        if dr:
            ok = row_there(dr < 0)
        if dc:
            beside = c > 0 if dc < 0 else c < n_col - 1
            ok = beside if ok is None else jnp.logical_and(ok, beside)
        return ok

    for up in (True, False):
        pl.when(row_there(up))(lambda up=up: row_copy(up).start())
    for index in range(8):
        pl.when(side_there(index))(lambda index=index: pack_copy(index).start())

    for copy in loads:
        copy.wait()

    for conv_ref, w2 in ((conv_one_ref, w2a), (conv_two_ref, w2b)):
        w = conv_ref[...]
        pad = jnp.zeros((ch, 3 * ch), BF16)
        w2[0:ch, :] = jnp.concatenate([w, pad], axis=1)
        w2[ch : 2 * ch, :] = jnp.concatenate([pad, w], axis=1)

    def fill(slot, side, center):
        left = jnp.where(lane == 0, 0.0, pltpu.roll(center, 1, 1))
        right = jnp.where(lane == cols - 1, 0.0, pltpu.roll(center, cols - 1, 1))
        base = slot * (3 * ch)
        if not isinstance(slot, int):
            base = pl.multiple_of(base, 3 * ch)
        where = slice(side * cols, (side + 1) * cols)
        for t, part in enumerate((left, center, right)):
            x3[pl.ds(base + t * ch, ch), where] = part.astype(BF16)

    def fill_rows(i, carry):
        for j in range(2):
            for side in range(2):
                s = i * 2 + j
                fill(s + 2 - 2 * side, side, xt[s + side * (half - 2)].astype(F32))
        return carry

    lax.fori_loop(0, half // 2 + 1, fill_rows, 0)

    def first_sums(i, carry):
        base = i * (6 * ch)
        out = i * (2 * ch)
        if not isinstance(i, int):
            base, out = pl.multiple_of(base, 6 * ch), pl.multiple_of(out, 2 * ch)
        raw[pl.ds(out, 2 * ch), :] = dot(w2a[...], x3[pl.ds(base, 12 * ch), :])
        return carry

    for i in range(1, half // 2):
        first_sums(i, 0)

    bias_one = column(bias_one_ref[...])
    bias_two = column(bias_two_ref[...])
    bias_two = jnp.concatenate([bias_two, bias_two], axis=0)

    for up in (True, False):

        @pl.when(row_there(up))
        def _(up=up):
            row_copy(up).wait_send()
            row_copy(not up).wait_recv()

        @pl.when(jnp.logical_not(row_there(up)))
        def _(up=up):
            rows_in[0 if up else 1] = jnp.zeros((2, ch, cols), BF16)

    for index in range(8):

        @pl.when(side_there(index))
        def _(index=index):
            back = SIDES.index((-SIDES[index][0], -SIDES[index][1]))
            pack_copy(index).wait_send()
            pack_copy(back).wait_recv()

        @pl.when(jnp.logical_not(side_there(index)))
        def _(index=index):
            packs_in[index] = jnp.zeros((ch, cols), BF16)

    at_left = lax.rem(lane, 4) == 0

    def turned(x, shift):
        return pltpu.roll(x, shift % cols, 1)

    def rim(dr):
        left = packs_in[SIDES.index((dr, -1))].astype(F32)
        right = packs_in[SIDES.index((dr, 1))].astype(F32)
        mid = packs_in[SIDES.index((dr, 0))].astype(F32) if dr else packed
        return (
            jnp.where(at_left, turned(left, 2), mid),
            jnp.where(at_left, turned(left, 1), turned(right, -1)),
            jnp.where(at_left, mid, turned(right, -2)),
        )

    above, beside, below = rim(-1), rim(0), rim(1)

    for j in range(2):
        fill(j, 0, rows_in[0, j].astype(F32))
        fill(half + 2 + j, 1, rows_in[1, j].astype(F32))
    first_sums(0, 0)
    first_sums(half // 2, 0)

    row_of = lax.rem(lane + 1, cols) // 4
    first_row, last_row = row_of == 0, row_of == rows - 1
    main, extra = [], []
    for t in range(3):
        up_above, up_own = turned(above[t], 4), turned(beside[t], 4)
        main.append(jnp.where(first_row, up_above, up_own))
        extra.append(jnp.where(last_row, up_above, up_own))
    for t in range(3):
        main.append(beside[t])
        extra.append(jnp.where(last_row, above[t], below[t]))
    for t in range(3):
        down_below, down_own = turned(below[t], -4), turned(beside[t], -4)
        main.append(jnp.where(last_row, down_below, down_own))
        extra.append(jnp.where(last_row, down_own, down_below))
    zero = jnp.zeros((ch, cols), F32)
    added = []
    for part in (main, extra):
        added.append([])
        for dy in range(3):
            mid = part[3 * dy + 1]
            added[-1] += [jnp.where(at_left, mid, 0.0), zero, jnp.where(at_left, 0.0, mid)]
    taps = [jnp.concatenate(part, axis=0).astype(BF16) for part in (main, extra, added[0], added[1])]
    edge = dot(conv_one_ref[...], jnp.concatenate(taps, axis=1))
    add_main, add_extra = edge[:, 2 * cols : 3 * cols], edge[:, 3 * cols :]
    edge = jnp.maximum(edge[:, : 2 * cols] + bias_one, 0.0)
    outside = jnp.logical_or(
        jnp.logical_and(at_left, c == 0), jnp.logical_and(jnp.logical_not(at_left), c == n_col - 1)
    )
    off_grid = jnp.logical_or(
        jnp.logical_and(last_row, r == 0), jnp.logical_and(jnp.logical_not(last_row), r == n_row - 1)
    )
    edge_main = jnp.where(outside, 0.0, edge[:, :cols])
    edge_extra = jnp.where(jnp.logical_or(outside, off_grid), 0.0, edge[:, cols:])

    ends = jnp.logical_or(lane == 0, lane == cols - 1)

    def put(pair, side, edges, adds, blank=None):
        base, out = pair * (6 * ch), pair * (2 * ch)
        if not isinstance(pair, int):
            base, out = pl.multiple_of(base, 6 * ch), pl.multiple_of(out, 2 * ch)
        where = slice(side * cols, (side + 1) * cols)
        for o in range(2):
            part = raw[pl.ds(out + o * ch, ch), where] + jnp.where(ends, adds[o], 0.0)
            part = jnp.maximum(part + bias_one, 0.0)
            if blank is not None and blank[0] == o:
                part = jnp.where(blank[1], 0.0, part)
            left = jnp.where(lane == 0, edges[o], pltpu.roll(part, 1, 1))
            right = jnp.where(lane == cols - 1, edges[o], pltpu.roll(part, cols - 1, 1))
            for t, piece in enumerate((left, part, right)):
                f3[pl.ds(base + (3 * o + t) * ch, ch), where] = piece.astype(BF16)

    def both(h):
        return [(turned(x, -4 * h), turned(x, -4 * (h + 1))) for x in (edge_main, add_main)]

    def joined(first, h_first, second, h_second):
        return [
            (turned(a, -4 * h_first), turned(b, -4 * h_second)) for a, b in zip(first, second)
        ]

    inner, outer = (edge_main, add_main), (edge_extra, add_extra)
    put(0, 0, *joined(outer, rows - 1, inner, 0), blank=(0, r == 0))
    put(0, 1, *both(half - 1))

    total = jnp.zeros((2 * ch, 2 * cols), F32)
    for i in range(1, half // 2 + 1):
        put(i, 0, *both(2 * i - 1))
        if i < half // 2:
            put(i, 1, *both(2 * i - 1 + half))
        else:
            put(i, 1, *joined(inner, rows - 1, outer, 0), blank=(1, r == n_row - 1))
        part = dot(w2b[...], f3[(i - 1) * (6 * ch) : (i + 1) * (6 * ch), :])
        total = total + jnp.maximum(part + bias_two, 0.0)
    total = total[:ch] + total[ch:]
    total = total[:, :cols] + total[:, cols:]
    high = total.astype(BF16)
    low = (total - high.astype(F32)).astype(BF16)
    local_count = pos_ref.shape[0]
    share = SLOT // local_count
    at = iota((SLOT, cols), 0) - local_count * lax.rem(me, share)
    pool = (iota((SLOT, cols), 1) // PATCH == at).astype(F32).astype(BF16)
    pooled = (dot_nt(pool, high) + dot_nt(pool, low)) * (1.0 / (PATCH * PATCH))
    shift = (iota((SLOT, local_count), 1) == at[:, :local_count]).astype(F32).astype(BF16)
    tokens = pooled + dot(shift, pos_ref[...])
    tokens = jnp.concatenate([tokens, jnp.zeros((SLOT, 128 - ch), F32)], axis=1).astype(BF16)
    token[...] = tokens
    gathered[pl.ds(pl.multiple_of(me * SLOT, SLOT), SLOT), :] = tokens

    def token_copy(i, j, sender):
        return pltpu.make_async_remote_copy(
            src_ref=token,
            dst_ref=gathered.at[pl.ds(pl.multiple_of(sender * SLOT, SLOT), SLOT)],
            send_sem=tok_send.at[i * n_col + j],
            recv_sem=tok_recv.at[sender],
            device_id=away(i, j),
            device_id_type=MESH,
        )

    def push(i, j, carry):
        token_copy(i, j, me).start()
        return carry

    def take(i, j, carry):
        token_copy(i, j, me).wait_send()
        rr, cc = away(i, j)
        token_copy(i, j, rr * n_col + cc).wait_recv()
        return carry

    others(push)

    pick = iota((owned, embed_ref.shape[0]), 1) == me * owned + iota((owned, embed_ref.shape[0]), 0)
    own = dot(pick.astype(F32).astype(BF16), embed_ref[...]).astype(BF16)
    query = dot(own, w_query_ref[...]).astype(BF16).astype(F32)
    tall = (HEADS * owned, e)
    own_head = iota(tall, 0) // owned == iota(tall, 1) // HEAD_DIM
    heads = jnp.where(own_head, jnp.concatenate([query] * HEADS, axis=0), 0.0).astype(BF16)
    wide = (visible_ref.shape[1], n * local_count)
    spread = iota(wide, 1) // local_count == iota(wide, 0)
    blocks = visible_ref.shape
    mine = iota(blocks, 0) == me * owned // QBLOCK
    seen_row = jnp.sum(jnp.where(mine, visible_ref[...], 0).astype(F32), axis=0, keepdims=True)
    seen = dot(
        jnp.broadcast_to(seen_row, (8, blocks[1])).astype(BF16), spread.astype(F32).astype(BF16)
    )[0:1] > 0.5

    others(take)

    every = gathered[...].astype(F32).reshape(n // share, share, SLOT, 128).sum(axis=1)
    every = every.reshape(n * local_count, 128).astype(BF16)[:, :ch]
    keys = dot(every, w_key_ref[...]).astype(BF16)
    values = dot(every, w_value_ref[...]).astype(BF16)
    score = dot_nt(heads, keys) * (1.0 / HEAD_DIM**0.5)
    peak = jnp.max(jnp.where(seen, score, -1e30), axis=1, keepdims=True)
    weight = jnp.where(seen, jnp.exp(score - peak), 0.0)
    norm = jnp.sum(weight, axis=1, keepdims=True)
    mixed = dot(weight.astype(BF16), values) / norm
    mixed = jnp.where(own_head, mixed, 0.0)
    attended = mixed[0:owned]
    for h in range(1, HEADS):
        attended = attended + mixed[h * owned : (h + 1) * owned]
    out_ref[...] = dot(attended.astype(BF16), w_out_ref[...]).astype(BF16)


def on_device(
    raster,
    conv_one,
    bias_one,
    conv_two,
    bias_two,
    pos_embed,
    query_embed,
    w_query,
    w_key,
    w_value,
    w_out,
    visible,
):
    ch, rows, cols = raster.shape
    n_row, n_col = lax.axis_size("row"), lax.axis_size("col")
    n = n_row * n_col
    owned = query_embed.shape[0] // n
    e = query_embed.shape[1]
    dma = pltpu.SemaphoreType.DMA
    operands = (
        raster,
        conv_one,
        bias_one.reshape(1, ch),
        conv_two,
        bias_two.reshape(1, ch),
        pos_embed.transpose(1, 2, 0).reshape(-1, ch),
        query_embed,
        w_query,
        w_key,
        w_value,
        w_out,
        visible,
    )
    operands = tuple(pltpu.with_memory_space_constraint(x, pltpu.HBM) for x in operands)
    wide = 3 * ch, 2 * cols
    return pl.pallas_call(
        functools.partial(kernel, (n_row, n_col, ch, rows, cols)),
        out_shape=jax.ShapeDtypeStruct((owned, e), BF16),
        in_specs=[pl.BlockSpec(memory_space=pltpu.HBM)] * len(operands),
        out_specs=pl.BlockSpec(memory_space=pltpu.VMEM),
        scratch_shapes=[pltpu.VMEM(x.shape, x.dtype) for x in operands]
        + [
            pltpu.VMEM((rows, ch, cols), BF16),
            pltpu.VMEM(((rows // 2 + 4) * wide[0], wide[1]), BF16),
            pltpu.VMEM(((rows // 4 + 1) * 2 * ch, 2 * cols), F32),
            pltpu.VMEM(((rows // 2 + 2) * wide[0], wide[1]), BF16),
            pltpu.VMEM((2 * ch, 12 * ch), BF16),
            pltpu.VMEM((2 * ch, 12 * ch), BF16),
            pltpu.VMEM((ch, cols), BF16),
            pltpu.VMEM((2, 2, ch, cols), BF16),
            pltpu.VMEM((8, ch, cols), BF16),
            pltpu.VMEM((SLOT, 128), BF16),
            pltpu.VMEM((n * SLOT, 128), BF16),
            dma((len(operands) + 3,)),
            dma((2,)),
            dma((2,)),
            dma((8,)),
            dma((8,)),
            dma((n,)),
            dma((n,)),
        ],
        compiler_params=pltpu.CompilerParams(
            collective_id=0, has_side_effects=True, vmem_limit_bytes=32 * 1024 * 1024
        ),
        cost_estimate=pl.CostEstimate(flops=1_000_000_000, bytes_accessed=2_000_000, transcendentals=0),
    )(*operands)


def solution(mesh):
    tile = P(None, "row", "col")
    in_specs = (tile, P(), P(), P(), P(), tile, P(), P(), P(), P(), P(), P())
    return jax.shard_map(
        on_device,
        mesh=mesh,
        in_specs=in_specs,
        out_specs=P(("row", "col"), None),
        check_vma=False,
    )
```
